128 devices in a mesh: row: 8 (over x, z_lo), col: 16 (over z_hi, y, core).
Axes of the slice: x: 4, y: 4, z: 4 (z_hi: 2, z_lo: 2; z = z_hi * 2 + z_lo), core: 2. Of those that a mesh axis runs over, the one named last changes fastest.
Arguments:
- object_field: float32 [2, 2, 4096, 8192], P(None, None, 'row', 'col'), may hold values from -4 to 4
- probe: float32 [2, 256, 256], replicated, may hold values from -5 to 5
- measured: float32 [1024, 256, 256], P(('row', 'col')), may hold values from 0.2 to 4
- offsets: int32 [1024, 2], P(('row', 'col')), may hold values from 0 to 511, as said below
- counts: int32 [128], P(('row', 'col')), may hold values from 1 to 8, as said below
Outputs:
- object_grad: float32 [2, 2, 4096, 8192], P(None, None, 'row', 'col')
- probe_grad: float32 [2, 256, 256], replicated
The draws below stay inside these ranges and needn't reach their ends.
Inputs may be any that keep to these rules, and one draw needn't show every extreme that they name: Every patch of 256 x 256 pixels lies inside the object; offsets reach the largest value of their range. `counts`: some device has all 8 slots live in every draw.
All inputs are finite; a program needn't handle non-finite values.
Results may differ from the reference program's by a relative error of at most 0.00013.
Values sent between devices are 32-bit elements; how exact they have to be, the bound alone decides.
No kernel may reach another device: no remote copies, remote signals or barrier semaphores. Data moves between devices by JAX's collectives and lax.ppermute only.
A program may use at most 128 MiB of HBM per device.

```python
import math
import jax
import jax.numpy as jnp
from jax import lax

P_SIZE = 256
SLICES = 2
TH = 512
TW = 512
CAP = 8
NH = 4096
NW = 8192
SLOTS = 1024
N_ROW = 8
N_COL = 16


def draw_offsets(key, part):
    key = jax.random.fold_in(key, 1)
    slot_ids = jnp.arange(SLOTS, dtype=jnp.int32)
    device = slot_ids // CAP
    row_ids = device // N_COL
    col_ids = device % N_COL
    height = jnp.where(row_ids == N_ROW - 1, TH - P_SIZE + 1, TH)
    width = jnp.where(col_ids == N_COL - 1, TW - P_SIZE + 1, TW)
    random_bits = jax.random.randint(key, (SLOTS, 2), 0, 1 << 20)
    tops = random_bits[:, 0] % height
    lefts = random_bits[:, 1] % width
    first_slot = slot_ids % CAP == 0
    tops = jnp.where(first_slot, height - 1, tops)
    lefts = jnp.where(first_slot, width - 1, lefts)
    return jnp.stack([tops, lefts], axis=1).astype(jnp.int32)


def draw_counts(key, part):
    key = jax.random.fold_in(key, 2)
    total = N_ROW * N_COL
    drawn = jax.random.randint(key, (total,), 1, CAP + 1)
    busiest = jax.random.randint(jax.random.fold_in(key, 7), (), 0, total)
    return jnp.where(jnp.arange(total) == busiest, CAP, drawn).astype(jnp.int32)


def level_of(rng, shape, cuts, least, largest):
    gain = 1.0
    for dim, shards_of in cuts:
        draws = jax.random.uniform(jax.random.fold_in(jax.random.fold_in(rng, 6), dim), (shards_of,), jnp.float32, least / len(cuts), largest / len(cuts))
        gain = gain * jnp.repeat(jnp.exp(draws), shape[dim] // shards_of).reshape((-1,) + (1,) * (len(shape) - 1 - dim))
    return gain


def bell_draw(key, dims, scale, limit, split=(), kind=jnp.bfloat16):
    values = jax.random.normal(key, dims, jnp.float32) * scale
    if len(split) > 0:
        values = level_of(key, dims, split, -0.22, 0.18) * values
    return jnp.clip(values, min=-limit, max=limit).astype(kind)


def setup_inputs(seed: int = 0) -> dict:
    splits = jax.random.split(jax.random.key(seed), 6)
    return {
        "object_field": bell_draw(splits[0], (2, SLICES, NH, NW), 0.7, 4.0, ((2, 8), (3, 16)), jnp.float32),
        "probe": bell_draw(splits[1], (2, P_SIZE, P_SIZE), 1.0, 5.0, (), jnp.float32),
        "measured": jnp.clip(jnp.exp(math.log(4.0) - 2.9957323 * jax.random.uniform(splits[2], (SLOTS, P_SIZE, P_SIZE), jnp.float32) ** level_of(splits[2], (SLOTS, P_SIZE, P_SIZE), ((0, 128),), -0.2, 0.2)), 0.2, 4.0),
        "offsets": draw_offsets(jax.random.fold_in(splits[5], 71), 0),
        "counts": draw_counts(jax.random.fold_in(splits[5], 71), 0),
    }


fresnel = 40.0

def matmul(left, right):
    return jnp.dot(left, right, precision=lax.Precision.HIGHEST, preferred_element_type=jnp.float32)

def make_tables(pattern_side):
    indices = jnp.arange(pattern_side, dtype=jnp.int32)
    product = indices[:, None] * indices[None, :] % pattern_side
    angles = 2.0 * math.pi / pattern_side * product.astype(jnp.float32)
    scale = 1.0 / math.sqrt(pattern_side)
    cos_table = jnp.cos(angles) * scale
    sin_table = jnp.sin(angles) * scale
    freqs = (indices + pattern_side // 2) % pattern_side - pattern_side // 2
    squared = freqs * freqs
    phase = fresnel * math.pi / (pattern_side * pattern_side) * (squared[:, None] + squared[None, :]).astype(jnp.float32)
    return (cos_table, sin_table, jnp.cos(phase), jnp.sin(phase))

def transform(real_part, imag_part, mat_real, mat_imag):
    left_re = matmul(mat_real, real_part) - matmul(mat_imag, imag_part)
    left_im = matmul(mat_real, imag_part) + matmul(mat_imag, real_part)
    out_re = matmul(left_re, mat_real) - matmul(left_im, mat_imag)
    out_im = matmul(left_re, mat_imag) + matmul(left_im, mat_real)
    return (out_re, out_im)

def slot_loss(sample_patch, probe, pattern, weight, tables):
    cos_table, sin_table, prop_re, prop_im = tables
    wave_re = probe[0] * sample_patch[0, 0] - probe[1] * sample_patch[1, 0]
    wave_im = probe[0] * sample_patch[1, 0] + probe[1] * sample_patch[0, 0]
    for layer in range(1, sample_patch.shape[1]):
        freq_re, freq_im = transform(wave_re, wave_im, cos_table, -sin_table)
        moved_re = freq_re * prop_re - freq_im * prop_im
        moved_im = freq_re * prop_im + freq_im * prop_re
        back_re, back_im = transform(moved_re, moved_im, cos_table, sin_table)
        wave_re = back_re * sample_patch[0, layer] - back_im * sample_patch[1, layer]
        wave_im = back_re * sample_patch[1, layer] + back_im * sample_patch[0, layer]
    far_re, far_im = transform(wave_re, wave_im, cos_table, -sin_table)
    misfit = far_re * far_re + far_im * far_im - pattern
    return 0.5 * weight * jnp.sum(misfit * misfit)

def reference(object_field, probe, measured, offsets, counts):
    pattern_side = probe.shape[1]
    tables = make_tables(pattern_side)
    slot_ids = jnp.arange(SLOTS, dtype=jnp.int32)
    device = slot_ids // CAP
    row_ids = device // N_COL
    col_ids = device % N_COL
    tops = (row_ids * TH + offsets[:, 0]).astype(jnp.int32)
    lefts = (col_ids * TW + offsets[:, 1]).astype(jnp.int32)
    weights = (slot_ids % CAP < counts[device]).astype(jnp.float32)

    def visit(carry, inputs):
        grid, probe_total = carry
        top, left, pattern, weight = inputs
        start = (jnp.int32(0), jnp.int32(0), top, left)
        sample_patch = lax.dynamic_slice(object_field, start, (2, SLICES, pattern_side, pattern_side))

        def local_loss(patch_arg, probe_arg):
            return slot_loss(patch_arg, probe_arg, pattern, weight, tables)
        unused, pull = jax.vjp(local_loss, sample_patch, probe)
        patch_grad, probe_term = pull(jnp.ones((), jnp.float32))
        current = lax.dynamic_slice(grid, start, (2, SLICES, pattern_side, pattern_side))
        grid = lax.dynamic_update_slice(grid, current + patch_grad, start)
        return ((grid, probe_total + probe_term), None)
    init = (jnp.zeros_like(object_field), jnp.zeros_like(probe))
    (grid, probe_total), unused = lax.scan(visit, init, (tops, lefts, measured, weights))
    return (grid, probe_total)
```

```python
import math

import jax
import jax.numpy as jnp
import ml_dtypes
import numpy as np
from jax import lax
from jax.experimental import pallas as pl
from jax.experimental.pallas import tpu as pltpu
from jax.sharding import PartitionSpec as P

fresnel = 40.0


def passed_along(shard, axis, by):
    length = lax.axis_size(axis)
    pairs = [(i, i + by) for i in range(length) if 0 <= i + by < length]
    return lax.ppermute(shard, axis, pairs)


def real_form(matrix):
    return np.block([[matrix.real, -matrix.imag], [matrix.imag, matrix.real]])


def make_tables(side):
    half = side // 2
    index = np.arange(side)
    dft = np.exp(-2j * np.pi * ((index[:, None] * index[None, :]) % side) / side) / math.sqrt(side)
    freqs = (index + half) % side - half
    chirp = np.exp(1j * fresnel * np.pi * (freqs * freqs) / (side * side))
    circulant = (dft.conj() * chirp[None, :]) @ dft
    near, far = circulant[:half, :half], circulant[:half, half:]
    mats = [real_form((near + far) / 2), real_form((near - far) / 2)]
    mats += [real_form(dft[0::2, :half]), real_form(dft[1::2, :half])]
    full = np.stack([mats[0], mats[1], mats[0].T, mats[1].T, mats[2], mats[3], mats[2].T, mats[3].T])
    full = full.astype(np.float32)
    high = full.astype(ml_dtypes.bfloat16)
    low = (full - high.astype(np.float32)).astype(ml_dtypes.bfloat16)
    return np.stack([high, low], axis=1)


def split(x):
    high = x.astype(jnp.bfloat16)
    return high, (x - high.astype(jnp.float32)).astype(jnp.bfloat16)


def dot(a, b):
    return jnp.dot(a, b, preferred_element_type=jnp.float32)


def fold(x):
    half = x.shape[0] // 2
    rows = (x[:half] + x[half:], x[:half] - x[half:])
    return [(r[:, :half] + r[:, half:], r[:, :half] - r[:, half:]) for r in rows]


def unfold(quads):
    (uu, uv), (vu, vv) = quads
    rows_u = jnp.concatenate([uu + uv, uu - uv], axis=1)
    rows_v = jnp.concatenate([vu + vv, vu - vv], axis=1)
    return jnp.concatenate([rows_u + rows_v, rows_u - rows_v], axis=0)


def two_sided(quads_re, quads_im, tables, left, right):
    half = quads_re[0][0].shape[0]
    lefts = []
    for p in range(2):
        z = jnp.concatenate(
            [jnp.concatenate(quads_re[p], axis=1), jnp.concatenate(quads_im[p], axis=1)], axis=0
        )
        z_hi, z_lo = split(z)
        m_hi, m_lo = tables[left + p, 0], tables[left + p, 1]
        lefts.append(
            dot(
                jnp.concatenate([m_hi, m_hi, m_lo], axis=1),
                jnp.concatenate([z_hi, z_lo, z_hi], axis=0),
            )
        )
    out_re = [[None, None], [None, None]]
    out_im = [[None, None], [None, None]]
    for q in range(2):
        cols = slice(q * half, (q + 1) * half)
        v = jnp.concatenate(
            [jnp.concatenate([w[:half, cols], w[half:, cols]], axis=1) for w in lefts], axis=0
        )
        v_hi, v_lo = split(v)
        m_hi, m_lo = tables[right + q, 0], tables[right + q, 1]
        y = dot(
            jnp.concatenate([v_hi, v_hi, v_lo], axis=1),
            jnp.concatenate([m_hi, m_lo, m_hi], axis=0),
        )
        for p in range(2):
            out_re[p][q] = y[p * half : (p + 1) * half, :half]
            out_im[p][q] = y[p * half : (p + 1) * half, half:]
    return out_re, out_im


def whole(quads):
    return jnp.concatenate([jnp.concatenate(r, axis=1) for r in quads], axis=0)


def quarters(x):
    half = x.shape[0] // 2
    return [(r[:, :half], r[:, half:]) for r in (x[:half], x[half:])]


LANES = 128
ROWS = 8


def gradient_kernel(
    offsets, counts, obj, right, lower, corner, probe, measured, tables,
    main_out, right_out, corner_out, lower_out, probe_out,
    ext, grid,
):
    side = probe.shape[1]
    height, width = obj.shape[2], obj.shape[3]
    layers = obj.shape[1]
    ext[:, :, :height, :width] = obj[...]
    ext[:, :, :height, width:] = right[...]
    ext[:, :, height:, :width] = lower[...]
    ext[:, :, height:, width:] = corner[...]
    grid[...] = jnp.zeros_like(grid)
    probe_out[...] = jnp.zeros_like(probe_out)
    blocks, tiles = side // LANES, side // ROWS
    lane = lax.broadcasted_iota(jnp.int32, (tiles, ROWS, LANES), 2)
    row = lax.broadcasted_iota(jnp.int32, (tiles, ROWS, LANES), 1)
    row_more = lax.broadcasted_iota(jnp.int32, (tiles + 1, ROWS, LANES), 1)

    def place(part, layer, top, edge, k):
        first = pl.multiple_of(top // ROWS * ROWS, ROWS)
        start = pl.multiple_of(edge // LANES * LANES + k * LANES, LANES)
        return (part, layer, pl.ds(first, side + ROWS), pl.ds(start, LANES))

    def patch(part, layer, top, edge):
        down, over = top % ROWS, edge % LANES
        turned = []
        for k in range(blocks + 1):
            x = ext[place(part, layer, top, edge, k)].reshape(tiles + 1, ROWS, LANES)
            x = pltpu.roll(x, (ROWS - down) % ROWS, 1)
            x = jnp.where(row < ROWS - down, x[:-1], x[1:])
            turned.append(pltpu.roll(x, (LANES - over) % LANES, 2))
        keep = lane < LANES - over
        return jnp.concatenate(
            [jnp.where(keep, turned[k], turned[k + 1]).reshape(side, LANES) for k in range(blocks)], axis=1
        )

    def add_patch(part, layer, top, edge, value):
        down, over = top % ROWS, edge % LANES
        turned = []
        zero = jnp.zeros((tiles, ROWS, LANES), jnp.float32)
        none = jnp.zeros((1, ROWS, LANES), jnp.float32)
        for k in range(blocks):
            x = value[:, k * LANES : (k + 1) * LANES].reshape(tiles, ROWS, LANES)
            turned.append(pltpu.roll(x, over, 2))
        for k in range(blocks + 1):
            after = turned[k] if k < blocks else zero
            before = turned[k - 1] if k > 0 else zero
            x = pltpu.roll(jnp.where(lane >= over, after, before), down, 1)
            x = jnp.where(
                row_more >= down, jnp.concatenate([x, none], axis=0), jnp.concatenate([none, x], axis=0)
            )
            at = place(part, layer, top, edge, k)
            grid[at] = grid[at] + x.reshape(side + ROWS, LANES)

    def visit(slot, carry):
        top = offsets[slot, 0]
        where = (top, offsets[slot, 1])

        p_re, p_im = probe[0], probe[1]
        a_re, a_im = patch(0, 0, *where), patch(1, 0, *where)
        psi_re = p_re * a_re - p_im * a_im
        psi_im = p_re * a_im + p_im * a_re
        y_re, y_im = two_sided(fold(psi_re), fold(psi_im), tables, 0, 2)
        phi_re, phi_im = unfold(y_re), unfold(y_im)

        b_re, b_im = patch(0, 1, *where), patch(1, 1, *where)
        psi_re = phi_re * b_re - phi_im * b_im
        psi_im = phi_re * b_im + phi_im * b_re
        y_re, y_im = two_sided(fold(psi_re), fold(psi_im), tables, 4, 6)
        far_re, far_im = whole(y_re), whole(y_im)
        misfit = 2.0 * (far_re * far_re + far_im * far_im - measured[slot])
        y_re, y_im = two_sided(quarters(misfit * far_re), quarters(misfit * far_im), tables, 6, 4)
        d_re, d_im = unfold(y_re), unfold(y_im)
        add_patch(0, 1, *where, phi_re * d_re + phi_im * d_im)
        add_patch(1, 1, *where, phi_re * d_im - phi_im * d_re)

        e_re = b_re * d_re + b_im * d_im
        e_im = b_re * d_im - b_im * d_re
        y_re, y_im = two_sided(fold(e_re), fold(e_im), tables, 2, 0)
        d_re, d_im = unfold(y_re), unfold(y_im)
        add_patch(0, 0, *where, p_re * d_re + p_im * d_im)
        add_patch(1, 0, *where, p_re * d_im - p_im * d_re)
        a_re, a_im = patch(0, 0, *where), patch(1, 0, *where)
        probe_out[0] += a_re * d_re + a_im * d_im
        probe_out[1] += a_re * d_im - a_im * d_re
        return carry

    lax.fori_loop(0, jnp.minimum(counts[0], measured.shape[0]), visit, 0)
    main_out[...] = grid[:, :, :height, :width]
    right_out[...] = grid[:, :, :height, width:]
    lower_out[...] = grid[:, :, height:, :width]
    corner_out[...] = grid[:, :, height:, width:]


def sum_over_all(value):
    rows, cols = lax.axis_size("row"), lax.axis_size("col")
    flat = value.reshape(cols, -1, LANES)
    share = jnp.sum(lax.all_to_all(flat, "col", 0, 0, tiled=True), axis=0)
    share = jnp.sum(lax.all_to_all(share.reshape(rows, -1, LANES), "row", 0, 0, tiled=True), axis=0)
    share = lax.all_to_all(jnp.broadcast_to(share, (rows, *share.shape)), "row", 0, 0, tiled=True)
    share = share.reshape(-1, LANES)
    share = lax.all_to_all(jnp.broadcast_to(share, (cols, *share.shape)), "col", 0, 0, tiled=True)
    return share.reshape(value.shape)


def per_device(object_field, probe, measured, offsets, counts):
    _, layers, height, width = object_field.shape
    side = probe.shape[1]
    slots_here = measured.shape[0]

    lower_left = passed_along(object_field[:, :, :side, :side], "row", -1)
    right_rim = passed_along(object_field[:, :, :, :side], "col", -1)
    lower_right = passed_along(object_field[:, :, :side, side:], "row", -1)
    corner = passed_along(lower_left, "col", -1)
    lower = jnp.concatenate([lower_left, lower_right], axis=3)

    order = np.concatenate([np.arange(0, side, 2), np.arange(1, side, 2)])
    picks = jnp.asarray(np.eye(side, dtype=np.float32)[order])
    pattern = jnp.einsum("qab,db->qad", measured, picks, precision=lax.Precision.HIGHEST)
    pattern = jnp.einsum("ca,qad->qcd", picks, pattern, precision=lax.Precision.HIGHEST)
    tables = jnp.asarray(make_tables(side))

    f32 = jnp.float32
    vmem = pl.BlockSpec(memory_space=pltpu.VMEM)
    smem = pl.BlockSpec(memory_space=pltpu.SMEM)
    passes = 4 * 4 * 3 * slots_here
    main, right_grad, corner_grad, lower_grad, probe_terms = pl.pallas_call(
        gradient_kernel,
        in_specs=[smem, smem] + [vmem] * 7,
        out_specs=[vmem] * 5,
        out_shape=[
            jax.ShapeDtypeStruct((2, layers, height, width), f32),
            jax.ShapeDtypeStruct((2, layers, height, side), f32),
            jax.ShapeDtypeStruct((2, layers, side, side), f32),
            jax.ShapeDtypeStruct((2, layers, side, width), f32),
            jax.ShapeDtypeStruct((2, side, side), f32),
        ],
        scratch_shapes=[
            pltpu.VMEM((2, layers, height + side, width + side), f32),
            pltpu.VMEM((2, layers, height + side, width + side), f32),
        ],
        compiler_params=pltpu.CompilerParams(vmem_limit_bytes=60 * 1024 * 1024),
        cost_estimate=pl.CostEstimate(
            flops=passes * 2 * side**3, bytes_accessed=24 * 1024 * 1024, transcendentals=0
        ),
    )(offsets, counts, object_field, right_rim, lower, corner, probe, pattern, tables)

    down_right = passed_along(lower_grad[:, :, :, side:], "row", 1)
    from_corner = passed_along(corner_grad, "col", 1)
    from_left = passed_along(right_grad, "col", 1)
    down_left = passed_along(lower_grad[:, :, :, :side] + from_corner, "row", 1)
    probe_grad = sum_over_all(probe_terms)
    main = main.at[:, :, :, :side].add(from_left)
    main = main.at[:, :, :side, side:].add(down_right)
    main = main.at[:, :, :side, :side].add(down_left)
    return (main, probe_grad)


def solution(mesh):
    placed = (
        P(None, None, "row", "col"),
        P(),
        P(("row", "col"), None, None),
        P(("row", "col"), None),
        P(("row", "col")),
    )
    return jax.shard_map(
        per_device,
        mesh=mesh,
        in_specs=placed,
        out_specs=(P(None, None, "row", "col"), P()),
        check_vma=False,
    )
```

```python
import math

import jax
import jax.numpy as jnp
import ml_dtypes
import numpy as np
from jax import lax
from jax.experimental import pallas as pl
from jax.experimental.pallas import tpu as pltpu
from jax.sharding import PartitionSpec as P

fresnel = 40.0


def passed_along(shard, axis, by):
    length = lax.axis_size(axis)
    pairs = [(i, i + by) for i in range(length) if 0 <= i + by < length]
    return lax.ppermute(shard, axis, pairs)


def real_form(matrix):
    return np.block([[matrix.real, -matrix.imag], [matrix.imag, matrix.real]])


def make_tables(side):
    half = side // 2
    index = np.arange(side)
    dft = np.exp(-2j * np.pi * ((index[:, None] * index[None, :]) % side) / side) / math.sqrt(side)
    freqs = (index + half) % side - half
    chirp = np.exp(1j * fresnel * np.pi * (freqs * freqs) / (side * side))
    circulant = (dft.conj() * chirp[None, :]) @ dft
    near, far = circulant[:half, :half], circulant[:half, half:]
    mats = [real_form((near + far) / 2), real_form((near - far) / 2)]
    mats += [real_form(dft[0::2, :half]), real_form(dft[1::2, :half])]
    full = np.stack([mats[0], mats[1], mats[0].T, mats[1].T, mats[2], mats[3], mats[2].T, mats[3].T])
    full = full.astype(np.float32)
    high = full.astype(ml_dtypes.bfloat16)
    low = (full - high.astype(np.float32)).astype(ml_dtypes.bfloat16)
    return np.stack([high, low], axis=1)


def split(x):
    high = x.astype(jnp.bfloat16)
    return high, (x - high.astype(jnp.float32)).astype(jnp.bfloat16)


def dot(a, b):
    return jnp.dot(a, b, preferred_element_type=jnp.float32)


def fold(x):
    half = x.shape[0] // 2
    rows = (x[:half] + x[half:], x[:half] - x[half:])
    return [(r[:, :half] + r[:, half:], r[:, :half] - r[:, half:]) for r in rows]


def unfold(quads):
    (uu, uv), (vu, vv) = quads
    rows_u = jnp.concatenate([uu + uv, uu - uv], axis=1)
    rows_v = jnp.concatenate([vu + vv, vu - vv], axis=1)
    return jnp.concatenate([rows_u + rows_v, rows_u - rows_v], axis=0)


def two_sided(quads_re, quads_im, tables, left, right):
    half = quads_re[0][0].shape[0]
    lefts = []
    for p in range(2):
        z = jnp.concatenate(
            [jnp.concatenate(quads_re[p], axis=1), jnp.concatenate(quads_im[p], axis=1)], axis=0
        )
        z_hi, z_lo = split(z)
        m_hi, m_lo = tables[left + p, 0], tables[left + p, 1]
        lefts.append(
            dot(
                jnp.concatenate([m_hi, m_hi, m_lo], axis=1),
                jnp.concatenate([z_hi, z_lo, z_hi], axis=0),
            )
        )
    out_re = [[None, None], [None, None]]
    out_im = [[None, None], [None, None]]
    for q in range(2):
        cols = slice(q * half, (q + 1) * half)
        v = jnp.concatenate(
            [jnp.concatenate([w[:half, cols], w[half:, cols]], axis=1) for w in lefts], axis=0
        )
        v_hi, v_lo = split(v)
        m_hi, m_lo = tables[right + q, 0], tables[right + q, 1]
        y = dot(
            jnp.concatenate([v_hi, v_hi, v_lo], axis=1),
            jnp.concatenate([m_hi, m_lo, m_hi], axis=0),
        )
        for p in range(2):
            out_re[p][q] = y[p * half : (p + 1) * half, :half]
            out_im[p][q] = y[p * half : (p + 1) * half, half:]
    return out_re, out_im


def whole(quads):
    return jnp.concatenate([jnp.concatenate(r, axis=1) for r in quads], axis=0)


def quarters(x):
    half = x.shape[0] // 2
    return [(r[:, :half], r[:, half:]) for r in (x[:half], x[half:])]


LANES = 128
ROWS = 8
MIB = 1024 * 1024


def places(top, edge, side):
    first = pl.multiple_of(top // ROWS * ROWS, ROWS)
    start = pl.multiple_of(edge // LANES * LANES, LANES)
    return [(pl.ds(first, side + ROWS), pl.ds(pl.multiple_of(start + k * LANES, LANES), LANES)) for k in range(3)]


def iotas(rows):
    return (
        lax.broadcasted_iota(jnp.int32, (ROWS, LANES), 0),
        lax.broadcasted_iota(jnp.int32, (rows, LANES), 1),
    )


def window(ext, at, top, edge, side):
    down, over = top % ROWS, edge % LANES
    row, lane = iotas(side + ROWS)
    x = [ext[(*at, *place)] for place in places(top, edge, side)]
    blocks = [jnp.where(lane >= over, x[0], x[2]), x[1]]
    return jnp.concatenate(
        [
            jnp.concatenate([jnp.where(row >= down, y[:ROWS], y[side:]), y[ROWS:side]], axis=0)
            for y in blocks
        ],
        axis=1,
    )


def add_window(grid, at, top, edge, value):
    side = value.shape[0]
    down, over = top % ROWS, edge % LANES
    row, lane = iotas(side)
    x, y = value[:, :LANES], value[:, LANES:]
    blocks = [jnp.where(lane >= over, x, 0.0), y, jnp.where(lane < over, x, 0.0)]
    for place, block in zip(places(top, edge, side), blocks):
        low = jnp.where(row >= down, block[:ROWS], 0.0)
        high = jnp.where(row < down, block[:ROWS], 0.0)
        here = (*at, *place)
        grid[here] = grid[here] + jnp.concatenate([low, block[ROWS:], high], axis=0)


def turned(x, down, over):
    side = x.shape[0]
    tiles = side // ROWS
    row = lax.broadcasted_iota(jnp.int32, (tiles, ROWS, LANES), 1)
    lane = lax.broadcasted_iota(jnp.int32, (side, LANES), 1)
    blocks = []
    for k in range(2):
        y = pltpu.roll(x[:, k * LANES : (k + 1) * LANES].reshape(tiles, ROWS, LANES), down, 1)
        before = jnp.concatenate([y[-1:], y[:-1]], axis=0)
        blocks.append(pltpu.roll(jnp.where(row >= down, y, before).reshape(side, LANES), over, 1))
    return jnp.concatenate([jnp.where(lane >= over, blocks[k], blocks[1 - k]) for k in range(2)], axis=1)


def turned_back(x, down, over):
    side = x.shape[0]
    tiles = side // ROWS
    row = lax.broadcasted_iota(jnp.int32, (tiles, ROWS, LANES), 1)
    lane = lax.broadcasted_iota(jnp.int32, (side, LANES), 1)
    blocks = [pltpu.roll(x[:, k * LANES : (k + 1) * LANES], (LANES - over) % LANES, 1) for k in range(2)]
    out = []
    for k in range(2):
        y = jnp.where(lane < LANES - over, blocks[k], blocks[1 - k]).reshape(tiles, ROWS, LANES)
        y = pltpu.roll(y, (ROWS - down) % ROWS, 1)
        following = jnp.concatenate([y[1:], y[:1]], axis=0)
        out.append(jnp.where(row < ROWS - down, y, following).reshape(side, LANES))
    return jnp.concatenate(out, axis=1)


def gradient_kernel(
    offsets, counts, obj, right0, right1, lower, corner, middle, probe, measured, tables,
    main_out, right0_out, right1_out, low_left_out, low_right_out, corner_out, probe_out, ext, grid,
):
    height, width = obj.shape[2:]
    side = probe.shape[1]
    ext[:, :, :height, :width] = obj[...]
    ext[:, 0, :height, width:] = right0[...]
    ext[:, 1, :height, width:] = right1[...]
    ext[:, :, height:, :width] = lower[...]
    ext[:, :, height:, width:] = corner[...] + middle[...]
    grid[...] = jnp.zeros_like(grid)
    probe_out[...] = jnp.zeros_like(probe_out)

    def visit(slot, carry):
        top, edge = offsets[slot, 0], offsets[slot, 1]
        p_re, p_im = (turned(probe[i], top % ROWS, edge % LANES) for i in range(2))
        a_re, a_im = (window(ext, (i, 0), top, edge, side) for i in range(2))
        psi_re = p_re * a_re - p_im * a_im
        psi_im = p_re * a_im + p_im * a_re
        y_re, y_im = two_sided(fold(psi_re), fold(psi_im), tables, 0, 2)
        phi_re, phi_im = unfold(y_re), unfold(y_im)
        b_re, b_im = (window(ext, (i, 1), top, edge, side) for i in range(2))
        psi_re = phi_re * b_re - phi_im * b_im
        psi_im = phi_re * b_im + phi_im * b_re
        y_re, y_im = two_sided(fold(psi_re), fold(psi_im), tables, 4, 6)
        far_re, far_im = whole(y_re), whole(y_im)
        misfit = 2.0 * (far_re * far_re + far_im * far_im - measured[slot])
        y_re, y_im = two_sided(quarters(misfit * far_re), quarters(misfit * far_im), tables, 6, 4)
        d_re, d_im = unfold(y_re), unfold(y_im)
        add_window(grid, (0, 1), top, edge, phi_re * d_re + phi_im * d_im)
        add_window(grid, (1, 1), top, edge, phi_re * d_im - phi_im * d_re)
        e_re = b_re * d_re + b_im * d_im
        e_im = b_re * d_im - b_im * d_re
        y_re, y_im = two_sided(fold(e_re), fold(e_im), tables, 2, 0)
        d_re, d_im = unfold(y_re), unfold(y_im)
        add_window(grid, (0, 0), top, edge, p_re * d_re + p_im * d_im)
        add_window(grid, (1, 0), top, edge, p_re * d_im - p_im * d_re)
        probe_out[0] += turned_back(a_re * d_re + a_im * d_im, top % ROWS, edge % LANES)
        probe_out[1] += turned_back(a_re * d_im - a_im * d_re, top % ROWS, edge % LANES)
        return carry

    lax.fori_loop(0, jnp.minimum(counts[0], measured.shape[0]), visit, 0)
    main_out[...] = grid[:, :, :height, :width]
    right0_out[...] = grid[:, 0, :height, width:]
    right1_out[...] = grid[:, 1, :height, width:]
    low_left_out[...] = grid[:, :, height:, :side]
    low_right_out[...] = grid[:, :, height:, side:width]
    corner_out[...] = grid[:, :, height:, width:]


def side_kernel(held, left0, left1, out):
    for layer, left in enumerate((left0, left1)):

        @pl.when(layer == pl.program_id(1))
        def _():
            out[...] = held[...] + left[...]


def top_kernel(held, middle, low_left, low_right, out):
    side = low_right.shape[1]
    out[:, :side] = held[:, :side] + (low_left[...] + middle[...])
    out[:, side:] = held[:, side:] + low_right[...]


def order_kernel(measured, picks, out):
    def parts(x):
        high = x.astype(jnp.bfloat16)
        rest = x - high.astype(jnp.float32)
        return (high, *split(rest))

    rows = sum(dot(picks[...], x) for x in parts(measured[...]))
    out[...] = sum(
        lax.dot_general(x, picks[...], (((1,), (1,)), ((), ())), preferred_element_type=jnp.float32)
        for x in parts(rows)
    )


def add_kernel(*refs):
    *terms, out = refs
    out[...] = sum(term[...] for term in terms)


def own_kernel(mine, value, own, other):
    own[...] = value[mine[0]]
    other[...] = value[1 - mine[0]]


BESIDE = pl.CostEstimate(flops=0, bytes_accessed=400 * MIB, transcendentals=0)
SMALL = pl.CostEstimate(flops=0, bytes_accessed=1024, transcendentals=0)


def fixed(shape):
    return pl.BlockSpec(shape, lambda q: (0,) * len(shape))


def per_slot(*shape):
    return pl.BlockSpec((None, *shape), lambda q: (q,) + (0,) * len(shape))


SCALARS = pl.BlockSpec(memory_space=pltpu.SMEM)


def struct(*shape):
    return jax.ShapeDtypeStruct(shape, jnp.float32)


def moved(shard, pairs):
    cols = lax.axis_size("col")
    flat = [(a * cols + b, c * cols + d) for (a, b), (c, d) in pairs]
    return lax.ppermute(shard, ("row", "col"), flat)


def along_columns(shard, by, middle):
    rows, cols = lax.axis_size("row"), lax.axis_size("col")
    cut, end = cols // 2, 0 if by < 0 else cols - 1
    first, second = (cut, cut - 1) if by < 0 else (cut - 1, cut)
    pairs = [(c, c + by) for c in range(cols) if c not in (first, end)]
    pairs += [(first, second)] if middle == "direct" else []
    pairs = [((r, c), (r, to)) for r in range(rows) for c, to in pairs]
    pairs += [((r ^ 1, end), (r, second)) for r in range(rows)] if middle == "relay" else []
    return moved(shard, pairs)


def to_end(shard, by):
    rows, cols = lax.axis_size("row"), lax.axis_size("col")
    first, end = (cols // 2, 0) if by < 0 else (cols // 2 - 1, cols - 1)
    return moved(shard, [((r, first), (r ^ 1, end)) for r in range(rows)])


def across_middle(shard, by):
    rows, cols = lax.axis_size("row"), lax.axis_size("col")
    first, second = (cols // 2, cols // 2 - 1) if by < 0 else (cols // 2 - 1, cols // 2)
    return moved(shard, [((r, first), (r + by, second)) for r in range(rows) if 0 <= r + by < rows])


def after(first, then):
    return lax.optimization_barrier((first, then))


PHYSICAL = {"core": 2, "y": 4, "x": 4, "z_lo": 2, "z_hi": 2}


def physical(r, c):
    return {"x": r // 2, "z_lo": r % 2, "z_hi": c // 8, "y": c // 2 % 4, "core": c % 2}


def exchanged(shard, **flips):
    pairs = []
    for r in range(lax.axis_size("row")):
        for c in range(lax.axis_size("col")):
            to = physical(r, c)
            for which, flip in flips.items():
                to[which] ^= flip
            pairs.append(((r, c), (to["x"] * 2 + to["z_lo"], to["z_hi"] * 8 + to["y"] * 2 + to["core"])))
    return moved(shard, pairs)


def added(*terms):
    return pl.pallas_call(add_kernel, out_shape=struct(*terms[0].shape), cost_estimate=BESIDE)(*terms)


def halved(bit, value):
    return pl.pallas_call(
        own_kernel, in_specs=[SCALARS, pl.BlockSpec(memory_space=pltpu.VMEM)],
        out_shape=[struct(*value.shape[1:])] * 2, cost_estimate=BESIDE,
    )(bit.reshape(1), value)


def split_rows(value, bit):
    first, second = value[: value.shape[0] // 2], value[value.shape[0] // 2 :]
    return jnp.where(bit == 1, second, first), jnp.where(bit == 1, first, second)


def joined(bit, own, other):
    return jnp.concatenate([jnp.where(bit == 1, other, own), jnp.where(bit == 1, own, other)], axis=0)


def per_device(object_field, probe, measured, offsets, counts):
    _, layers, height, width = object_field.shape
    side = probe.shape[1]
    slots = measured.shape[0]
    cols = lax.axis_size("col")
    cut = cols // 2

    here = lax.axis_index("col")
    wait = lax.optimization_barrier
    lower = passed_along(object_field[:, :, :side], "row", -1)
    rim = [object_field[:, i, :, :side] for i in range(layers)]
    half = to_end(rim[1], -1)
    right0 = along_columns(rim[0], -1, "direct")
    right1 = along_columns(jnp.where(here == 0, half, rim[1]), -1, "relay")
    middle = across_middle(object_field[:, :, :side, :side], -1)
    order = np.concatenate([np.arange(0, side, 2), np.arange(1, side, 2)])
    picks = jnp.asarray(np.eye(side)[order].astype(ml_dtypes.bfloat16))
    pattern = pl.pallas_call(
        order_kernel, grid=(slots,), in_specs=[per_slot(side, side), fixed((side, side))],
        out_specs=per_slot(side, side), out_shape=struct(slots, side, side), cost_estimate=BESIDE,
    )(measured, picks)
    pattern, lower = wait((pattern, lower))
    corner = along_columns(lower[:, :, :, :side], -1, "nothing")

    vmem = pl.BlockSpec(memory_space=pltpu.VMEM)
    extended = pltpu.VMEM((2, layers, height + side, width + side), jnp.float32)
    main, rim0, rim1, low_left, low_right, corner, probe_terms = pl.pallas_call(
        gradient_kernel,
        in_specs=[SCALARS, SCALARS] + [vmem] * 9,
        out_specs=[vmem] * 7,
        out_shape=[
            struct(2, layers, height, width), struct(2, height, side), struct(2, height, side),
            *[struct(2, layers, side, side)] * 3, struct(2, side, side),
        ],
        scratch_shapes=[extended, extended],
        compiler_params=pltpu.CompilerParams(vmem_limit_bytes=60 * MIB),
        cost_estimate=BESIDE,
    )(
        offsets, counts, object_field, right0, right1, lower, corner, middle, probe, pattern,
        jnp.asarray(make_tables(side)),
    )

    me = physical(lax.axis_index("row"), lax.axis_index("col"))
    low_bit, high_bit = me["y"] % 2 ^ me["y"] // 2, me["y"] // 2
    down_right = passed_along(low_right, "row", 1)
    from_corner = along_columns(corner, 1, "nothing")
    half = to_end(rim1, 1)
    own, other = halved(me["core"], probe_terms)
    own, other = split_rows(own + exchanged(other, core=1), low_bit)
    own, other = split_rows(own + exchanged(other, y=1), high_bit)
    arrived, down_right, from_corner, half, rim0, rim1, corner = wait(
        (exchanged(other, y=3), down_right, from_corner, half, rim0, rim1, corner)
    )
    from_left0 = along_columns(rim0, 1, "direct")
    from_left1 = along_columns(jnp.where(here == cols - 1, half, rim1), 1, "relay")
    middle = across_middle(corner, 1)
    share = own + arrived
    share = share + exchanged(share, x=1)
    share = share + exchanged(share, x=3)
    share = share + exchanged(share, z_lo=1)
    arrived, from_left0, from_left1, middle, low_left = wait(
        (exchanged(share, z_lo=1, z_hi=1), from_left0, from_left1, middle, low_left + from_corner)
    )
    down_left = passed_along(low_left, "row", 1)
    share = added(share, arrived)
    share = joined(high_bit, share, exchanged(share, y=3))
    share = joined(low_bit, share, exchanged(share, y=1))
    share, down_left = wait((share, down_left))
    probe_grad = joined(me["core"], share, exchanged(share, core=1)).reshape(probe.shape)

    edge = pl.BlockSpec((None, height, side), lambda i, j: (i, 0, 0))
    corner = pl.BlockSpec((None, None, side, side), lambda i, j: (i, j, 0, 0))
    upper = pl.BlockSpec((None, None, side, width), lambda i, j: (i, j, 0, 0))
    left = pl.BlockSpec((None, None, height, side), lambda i, j: (i, j, 0, 0))
    result = pl.pallas_call(
        side_kernel, grid=(2, layers), in_specs=[left, edge, edge], out_specs=left,
        out_shape=struct(*object_field.shape), input_output_aliases={0: 0}, cost_estimate=SMALL,
    )(main, from_left0, from_left1)
    result = pl.pallas_call(
        top_kernel, grid=(2, layers), in_specs=[upper, corner, corner, corner], out_specs=upper,
        out_shape=struct(*object_field.shape), input_output_aliases={0: 0},
    )(result, middle, down_left, down_right)
    return (result, probe_grad)


def solution(mesh):
    placed = (
        P(None, None, "row", "col"),
        P(),
        P(("row", "col"), None, None),
        P(("row", "col"), None),
        P(("row", "col")),
    )
    return jax.shard_map(
        per_device,
        mesh=mesh,
        in_specs=placed,
        out_specs=(P(None, None, "row", "col"), P()),
        check_vma=False,
    )
```

```python
import math

import jax
import jax.numpy as jnp
import ml_dtypes
import numpy as np
from jax import lax
from jax.experimental import pallas as pl
from jax.experimental.pallas import tpu as pltpu
from jax.sharding import PartitionSpec as P

fresnel = 40.0


def passed_along(shard, axis, by):
    length = lax.axis_size(axis)
    pairs = [(i, i + by) for i in range(length) if 0 <= i + by < length]
    return lax.ppermute(shard, axis, pairs)


def real_form(matrix):
    return np.block([[matrix.real, -matrix.imag], [matrix.imag, matrix.real]])


def make_tables(side):
    half = side // 2
    index = np.arange(side)
    dft = np.exp(-2j * np.pi * ((index[:, None] * index[None, :]) % side) / side) / math.sqrt(side)
    freqs = (index + half) % side - half
    chirp = np.exp(1j * fresnel * np.pi * (freqs * freqs) / (side * side))
    circulant = (dft.conj() * chirp[None, :]) @ dft
    near, far = circulant[:half, :half], circulant[:half, half:]
    mats = [real_form((near + far) / 2), real_form((near - far) / 2)]
    mats += [real_form(dft[0::2, :half]), real_form(dft[1::2, :half])]
    full = np.stack([mats[0], mats[1], mats[0].T, mats[1].T, mats[2], mats[3], mats[2].T, mats[3].T])
    full = full.astype(np.float32)
    high = full.astype(ml_dtypes.bfloat16)
    low = (full - high.astype(np.float32)).astype(ml_dtypes.bfloat16)
    return np.stack([high, low], axis=1)


def split(x):
    high = x.astype(jnp.bfloat16)
    return high, (x - high.astype(jnp.float32)).astype(jnp.bfloat16)


def dot(a, b):
    return jnp.dot(a, b, preferred_element_type=jnp.float32)


def fold(x):
    half = x.shape[0] // 2
    rows = (x[:half] + x[half:], x[:half] - x[half:])
    return [(r[:, :half] + r[:, half:], r[:, :half] - r[:, half:]) for r in rows]


def unfold(quads):
    (uu, uv), (vu, vv) = quads
    rows_u = jnp.concatenate([uu + uv, uu - uv], axis=1)
    rows_v = jnp.concatenate([vu + vv, vu - vv], axis=1)
    return jnp.concatenate([rows_u + rows_v, rows_u - rows_v], axis=0)


def two_sided(quads_re, quads_im, tables, left, right):
    half = quads_re[0][0].shape[0]
    lefts = []
    for p in range(2):
        z = jnp.concatenate(
            [jnp.concatenate(quads_re[p], axis=1), jnp.concatenate(quads_im[p], axis=1)], axis=0
        )
        z_hi, z_lo = split(z)
        m_hi, m_lo = tables[left + p, 0], tables[left + p, 1]
        lefts.append(
            dot(
                jnp.concatenate([m_hi, m_hi, m_lo], axis=1),
                jnp.concatenate([z_hi, z_lo, z_hi], axis=0),
            )
        )
    out_re = [[None, None], [None, None]]
    out_im = [[None, None], [None, None]]
    for q in range(2):
        cols = slice(q * half, (q + 1) * half)
        v = jnp.concatenate(
            [jnp.concatenate([w[:half, cols], w[half:, cols]], axis=1) for w in lefts], axis=0
        )
        v_hi, v_lo = split(v)
        m_hi, m_lo = tables[right + q, 0], tables[right + q, 1]
        y = dot(
            jnp.concatenate([v_hi, v_hi, v_lo], axis=1),
            jnp.concatenate([m_hi, m_lo, m_hi], axis=0),
        )
        for p in range(2):
            out_re[p][q] = y[p * half : (p + 1) * half, :half]
            out_im[p][q] = y[p * half : (p + 1) * half, half:]
    return out_re, out_im


def whole(quads):
    return jnp.concatenate([jnp.concatenate(r, axis=1) for r in quads], axis=0)


def quarters(x):
    half = x.shape[0] // 2
    return [(r[:, :half], r[:, half:]) for r in (x[:half], x[half:])]


LANES = 128
ROWS = 8
MIB = 1024 * 1024


def places(top, edge, side):
    first = pl.multiple_of(top // ROWS * ROWS, ROWS)
    start = pl.multiple_of(edge // LANES * LANES, LANES)
    return [(pl.ds(first, side + ROWS), pl.ds(pl.multiple_of(start + k * LANES, LANES), LANES)) for k in range(3)]


def iotas(rows):
    return (
        lax.broadcasted_iota(jnp.int32, (ROWS, LANES), 0),
        lax.broadcasted_iota(jnp.int32, (rows, LANES), 1),
    )


def window(ext, at, top, edge, side):
    down, over = top % ROWS, edge % LANES
    row, lane = iotas(side + ROWS)
    x = [ext[(*at, *place)] for place in places(top, edge, side)]
    blocks = [jnp.where(lane >= over, x[0], x[2]), x[1]]
    return jnp.concatenate(
        [
            jnp.concatenate([jnp.where(row >= down, y[:ROWS], y[side:]), y[ROWS:side]], axis=0)
            for y in blocks
        ],
        axis=1,
    )


def add_window(grid, at, top, edge, value):
    side = value.shape[0]
    down, over = top % ROWS, edge % LANES
    row, lane = iotas(side)
    x, y = value[:, :LANES], value[:, LANES:]
    blocks = [jnp.where(lane >= over, x, 0.0), y, jnp.where(lane < over, x, 0.0)]
    for place, block in zip(places(top, edge, side), blocks):
        low = jnp.where(row >= down, block[:ROWS], 0.0)
        high = jnp.where(row < down, block[:ROWS], 0.0)
        here = (*at, *place)
        grid[here] = grid[here] + jnp.concatenate([low, block[ROWS:], high], axis=0)


def turned(x, down, over):
    side = x.shape[0]
    tiles = side // ROWS
    row = lax.broadcasted_iota(jnp.int32, (tiles, ROWS, LANES), 1)
    lane = lax.broadcasted_iota(jnp.int32, (side, LANES), 1)
    blocks = []
    for k in range(2):
        y = pltpu.roll(x[:, k * LANES : (k + 1) * LANES].reshape(tiles, ROWS, LANES), down, 1)
        before = jnp.concatenate([y[-1:], y[:-1]], axis=0)
        blocks.append(pltpu.roll(jnp.where(row >= down, y, before).reshape(side, LANES), over, 1))
    return jnp.concatenate([jnp.where(lane >= over, blocks[k], blocks[1 - k]) for k in range(2)], axis=1)


def turned_back(x, down, over):
    side = x.shape[0]
    tiles = side // ROWS
    row = lax.broadcasted_iota(jnp.int32, (tiles, ROWS, LANES), 1)
    lane = lax.broadcasted_iota(jnp.int32, (side, LANES), 1)
    blocks = [pltpu.roll(x[:, k * LANES : (k + 1) * LANES], (LANES - over) % LANES, 1) for k in range(2)]
    out = []
    for k in range(2):
        y = jnp.where(lane < LANES - over, blocks[k], blocks[1 - k]).reshape(tiles, ROWS, LANES)
        y = pltpu.roll(y, (ROWS - down) % ROWS, 1)
        following = jnp.concatenate([y[1:], y[:1]], axis=0)
        out.append(jnp.where(row < ROWS - down, y, following).reshape(side, LANES))
    return jnp.concatenate(out, axis=1)


def gradient_kernel(
    offsets, counts, obj, right0, right1, low_left, low_right, corner, middle, probe, measured, tables,
    main_out, right0_out, right1_out, low_left_out, low_right_out, corner_out, probe_out, ext, grid,
):
    height, width = obj.shape[2:]
    side = probe.shape[1]
    ext[:, :, :height, :width] = obj[...]
    ext[:, 0, :height, width:] = right0[...]
    ext[:, 1, :height, width:] = right1[...]
    ext[:, :, height:, :side] = low_left[...]
    ext[:, :, height:, side:width] = low_right[...]
    ext[:, :, height:, width:] = corner[...] + middle[...]
    grid[...] = jnp.zeros_like(grid)
    probe_out[...] = jnp.zeros_like(probe_out)

    def visit(slot, carry):
        top, edge = offsets[slot, 0], offsets[slot, 1]
        p_re, p_im = (turned(probe[i], top % ROWS, edge % LANES) for i in range(2))
        a_re, a_im = (window(ext, (i, 0), top, edge, side) for i in range(2))
        psi_re = p_re * a_re - p_im * a_im
        psi_im = p_re * a_im + p_im * a_re
        y_re, y_im = two_sided(fold(psi_re), fold(psi_im), tables, 0, 2)
        phi_re, phi_im = unfold(y_re), unfold(y_im)
        b_re, b_im = (window(ext, (i, 1), top, edge, side) for i in range(2))
        psi_re = phi_re * b_re - phi_im * b_im
        psi_im = phi_re * b_im + phi_im * b_re
        y_re, y_im = two_sided(fold(psi_re), fold(psi_im), tables, 4, 6)
        far_re, far_im = whole(y_re), whole(y_im)
        misfit = 2.0 * (far_re * far_re + far_im * far_im - measured[slot])
        y_re, y_im = two_sided(quarters(misfit * far_re), quarters(misfit * far_im), tables, 6, 4)
        d_re, d_im = unfold(y_re), unfold(y_im)
        add_window(grid, (0, 1), top, edge, phi_re * d_re + phi_im * d_im)
        add_window(grid, (1, 1), top, edge, phi_re * d_im - phi_im * d_re)
        e_re = b_re * d_re + b_im * d_im
        e_im = b_re * d_im - b_im * d_re
        y_re, y_im = two_sided(fold(e_re), fold(e_im), tables, 2, 0)
        d_re, d_im = unfold(y_re), unfold(y_im)
        add_window(grid, (0, 0), top, edge, p_re * d_re + p_im * d_im)
        add_window(grid, (1, 0), top, edge, p_re * d_im - p_im * d_re)
        probe_out[0] += turned_back(a_re * d_re + a_im * d_im, top % ROWS, edge % LANES)
        probe_out[1] += turned_back(a_re * d_im - a_im * d_re, top % ROWS, edge % LANES)
        return carry

    lax.fori_loop(0, jnp.minimum(counts[0], measured.shape[0]), visit, 0)
    main_out[...] = grid[:, :, :height, :width]
    right0_out[...] = grid[:, 0, :height, width:]
    right1_out[...] = grid[:, 1, :height, width:]
    low_left_out[...] = grid[:, :, height:, :side]
    low_right_out[...] = grid[:, :, height:, side:width]
    corner_out[...] = grid[:, :, height:, width:]


def side_kernel(held, left0, left1, out):
    for layer, left in enumerate((left0, left1)):

        @pl.when(layer == pl.program_id(1))
        def _():
            out[...] = held[...] + left[...]


def top_kernel(held, middle, low_left, low_right, out):
    side = low_right.shape[1]
    out[:, :side] = held[:, :side] + (low_left[...] + middle[...])
    out[:, side:] = held[:, side:] + low_right[...]


def order_kernel(measured, picks, out):
    def parts(x):
        high = x.astype(jnp.bfloat16)
        rest = x - high.astype(jnp.float32)
        return (high, *split(rest))

    rows = sum(dot(picks[...], x) for x in parts(measured[...]))
    out[...] = sum(
        lax.dot_general(x, picks[...], (((1,), (1,)), ((), ())), preferred_element_type=jnp.float32)
        for x in parts(rows)
    )


def add_kernel(*refs):
    *terms, out = refs
    out[...] = sum(term[...] for term in terms)


def own_kernel(mine, value, own, other):
    own[...] = value[mine[0]]
    other[...] = value[1 - mine[0]]


BESIDE = pl.CostEstimate(flops=0, bytes_accessed=400 * MIB, transcendentals=0)
SMALL = pl.CostEstimate(flops=0, bytes_accessed=1024, transcendentals=0)


def fixed(shape):
    return pl.BlockSpec(shape, lambda q: (0,) * len(shape))


def per_slot(*shape):
    return pl.BlockSpec((None, *shape), lambda q: (q,) + (0,) * len(shape))


SCALARS = pl.BlockSpec(memory_space=pltpu.SMEM)


def struct(*shape):
    return jax.ShapeDtypeStruct(shape, jnp.float32)


def moved(shard, pairs):
    cols = lax.axis_size("col")
    flat = [(a * cols + b, c * cols + d) for (a, b), (c, d) in pairs]
    return lax.ppermute(shard, ("row", "col"), flat)


def along_columns(shard, by, middle):
    rows, cols = lax.axis_size("row"), lax.axis_size("col")
    cut, end = cols // 2, 0 if by < 0 else cols - 1
    first, second = (cut, cut - 1) if by < 0 else (cut - 1, cut)
    pairs = [(c, c + by) for c in range(cols) if c not in (first, end)]
    pairs += [(first, second)] if middle == "direct" else []
    pairs = [((r, c), (r, to)) for r in range(rows) for c, to in pairs]
    pairs += [((r ^ 1, end), (r, second)) for r in range(rows)] if middle == "relay" else []
    return moved(shard, pairs)


def to_end(shard, by):
    rows, cols = lax.axis_size("row"), lax.axis_size("col")
    first, end = (cols // 2, 0) if by < 0 else (cols // 2 - 1, cols - 1)
    return moved(shard, [((r, first), (r ^ 1, end)) for r in range(rows)])


def across_middle(shard, by):
    rows, cols = lax.axis_size("row"), lax.axis_size("col")
    first, second = (cols // 2, cols // 2 - 1) if by < 0 else (cols // 2 - 1, cols // 2)
    return moved(shard, [((r, first), (r + by, second)) for r in range(rows) if 0 <= r + by < rows])


def after(first, then):
    return lax.optimization_barrier((first, then))


PHYSICAL = {"core": 2, "y": 4, "x": 4, "z_lo": 2, "z_hi": 2}


def physical(r, c):
    return {"x": r // 2, "z_lo": r % 2, "z_hi": c // 8, "y": c // 2 % 4, "core": c % 2}


def exchanged(shard, **flips):
    pairs = []
    for r in range(lax.axis_size("row")):
        for c in range(lax.axis_size("col")):
            to = physical(r, c)
            for which, flip in flips.items():
                to[which] ^= flip
            pairs.append(((r, c), (to["x"] * 2 + to["z_lo"], to["z_hi"] * 8 + to["y"] * 2 + to["core"])))
    return moved(shard, pairs)


def added(*terms):
    return pl.pallas_call(add_kernel, out_shape=struct(*terms[0].shape), cost_estimate=BESIDE)(*terms)


def halved(bit, value):
    return pl.pallas_call(
        own_kernel, in_specs=[SCALARS, pl.BlockSpec(memory_space=pltpu.VMEM)],
        out_shape=[struct(*value.shape[1:])] * 2, cost_estimate=BESIDE,
    )(bit.reshape(1), value)


def split_rows(value, bit):
    first, second = value[: value.shape[0] // 2], value[value.shape[0] // 2 :]
    return jnp.where(bit == 1, second, first), jnp.where(bit == 1, first, second)


def joined(bit, own, other):
    return jnp.concatenate([jnp.where(bit == 1, other, own), jnp.where(bit == 1, own, other)], axis=0)


def per_device(object_field, probe, measured, offsets, counts):
    _, layers, height, width = object_field.shape
    side = probe.shape[1]
    slots = measured.shape[0]
    cols = lax.axis_size("col")
    cut = cols // 2

    here = lax.axis_index("col")
    wait = lax.optimization_barrier
    low_left = passed_along(object_field[:, :, :side, :side], "row", -1)
    low_right = passed_along(object_field[:, :, :side, side:], "row", -1)
    rim = [object_field[:, i, :, :side] for i in range(layers)]
    half = to_end(rim[1], -1)
    right0 = along_columns(rim[0], -1, "direct")
    right1 = along_columns(jnp.where(here == 0, half, rim[1]), -1, "relay")
    middle = across_middle(object_field[:, :, :side, :side], -1)
    order = np.concatenate([np.arange(0, side, 2), np.arange(1, side, 2)])
    picks = jnp.asarray(np.eye(side)[order].astype(ml_dtypes.bfloat16))
    pattern = pl.pallas_call(
        order_kernel, grid=(slots,), in_specs=[per_slot(side, side), fixed((side, side))],
        out_specs=per_slot(side, side), out_shape=struct(slots, side, side), cost_estimate=BESIDE,
    )(measured, picks)
    pattern, low_left = wait((pattern, low_left))
    corner = along_columns(low_left, -1, "nothing")

    vmem = pl.BlockSpec(memory_space=pltpu.VMEM)
    extended = pltpu.VMEM((2, layers, height + side, width + side), jnp.float32)
    main, rim0, rim1, low_left, low_right, corner, probe_terms = pl.pallas_call(
        gradient_kernel,
        in_specs=[SCALARS, SCALARS] + [vmem] * 10,
        out_specs=[vmem] * 7,
        out_shape=[
            struct(2, layers, height, width), struct(2, height, side), struct(2, height, side),
            *[struct(2, layers, side, side)] * 3, struct(2, side, side),
        ],
        scratch_shapes=[extended, extended],
        compiler_params=pltpu.CompilerParams(vmem_limit_bytes=60 * MIB),
        cost_estimate=BESIDE,
    )(
        offsets, counts, object_field, right0, right1, low_left, low_right, corner, middle, probe, pattern,
        jnp.asarray(make_tables(side)),
    )

    me = physical(lax.axis_index("row"), lax.axis_index("col"))
    low_bit, high_bit = me["y"] % 2 ^ me["y"] // 2, me["y"] // 2
    down_right = passed_along(low_right, "row", 1)
    from_corner = along_columns(corner, 1, "nothing")
    half = to_end(rim1, 1)
    own, other = halved(me["core"], probe_terms)
    own, other = split_rows(own + exchanged(other, core=1), low_bit)
    own, other = split_rows(own + exchanged(other, y=1), high_bit)
    from_left0 = along_columns(rim0, 1, "direct")
    arrived, down_right, corner = wait((exchanged(other, y=3), down_right, corner))
    from_left1 = along_columns(jnp.where(here == cols - 1, half, rim1), 1, "relay")
    middle = across_middle(corner, 1)
    share = own + arrived
    share = share + exchanged(share, x=1)
    share = share + exchanged(share, x=3)
    share = share + exchanged(share, z_lo=1)
    arrived, from_left0, from_left1, middle, low_left = wait(
        (exchanged(share, z_lo=1, z_hi=1), from_left0, from_left1, middle, low_left + from_corner)
    )
    down_left = passed_along(low_left, "row", 1)
    share = added(share, arrived)
    share = joined(high_bit, share, exchanged(share, y=3))
    share = joined(low_bit, share, exchanged(share, y=1))
    edge = pl.BlockSpec((None, height, side), lambda i, j: (i, 0, 0))
    corner = pl.BlockSpec((None, None, side, side), lambda i, j: (i, j, 0, 0))
    upper = pl.BlockSpec((None, None, side, width), lambda i, j: (i, j, 0, 0))
    left = pl.BlockSpec((None, None, height, side), lambda i, j: (i, j, 0, 0))
    result = pl.pallas_call(
        side_kernel, grid=(2, layers), in_specs=[left, edge, edge], out_specs=left,
        out_shape=struct(*object_field.shape), input_output_aliases={0: 0}, cost_estimate=SMALL,
    )(main, from_left0, from_left1)
    share, down_left, result = wait((share, down_left, result))
    probe_grad = joined(me["core"], share, exchanged(share, core=1)).reshape(probe.shape)
    result = pl.pallas_call(
        top_kernel, grid=(2, layers), in_specs=[upper, corner, corner, corner], out_specs=upper,
        out_shape=struct(*object_field.shape), input_output_aliases={0: 0},
    )(result, middle, down_left, down_right)
    return (result, probe_grad)


def solution(mesh):
    placed = (
        P(None, None, "row", "col"),
        P(),
        P(("row", "col"), None, None),
        P(("row", "col"), None),
        P(("row", "col")),
    )
    return jax.shard_map(
        per_device,
        mesh=mesh,
        in_specs=placed,
        out_specs=(P(None, None, "row", "col"), P()),
        check_vma=False,
    )
```

```python
import math

import jax
import jax.numpy as jnp
import ml_dtypes
import numpy as np
from jax import lax
from jax.experimental import pallas as pl
from jax.experimental.pallas import tpu as pltpu
from jax.sharding import PartitionSpec as P

fresnel = 40.0


def passed_along(shard, axis, by):
    length = lax.axis_size(axis)
    pairs = [(i, i + by) for i in range(length) if 0 <= i + by < length]
    return lax.ppermute(shard, axis, pairs)


def real_form(matrix):
    return np.block([[matrix.real, -matrix.imag], [matrix.imag, matrix.real]])


def make_tables(side):
    half = side // 2
    index = np.arange(side)
    dft = np.exp(-2j * np.pi * ((index[:, None] * index[None, :]) % side) / side) / math.sqrt(side)
    freqs = (index + half) % side - half
    chirp = np.exp(1j * fresnel * np.pi * (freqs * freqs) / (side * side))
    circulant = (dft.conj() * chirp[None, :]) @ dft
    near, far = circulant[:half, :half], circulant[:half, half:]
    mats = [real_form((near + far) / 2), real_form((near - far) / 2)]
    mats += [real_form(dft[0::2, :half]), real_form(dft[1::2, :half])]
    full = np.stack([mats[0], mats[1], mats[0].T, mats[1].T, mats[2], mats[3], mats[2].T, mats[3].T])
    full = full.astype(np.float32)
    high = full.astype(ml_dtypes.bfloat16)
    low = (full - high.astype(np.float32)).astype(ml_dtypes.bfloat16)
    return np.stack([high, low], axis=1)


def split(x):
    high = x.astype(jnp.bfloat16)
    return high, (x - high.astype(jnp.float32)).astype(jnp.bfloat16)


def dot(a, b):
    return jnp.dot(a, b, preferred_element_type=jnp.float32)


def fold(x):
    half = x.shape[0] // 2
    rows = (x[:half] + x[half:], x[:half] - x[half:])
    return [(r[:, :half] + r[:, half:], r[:, :half] - r[:, half:]) for r in rows]


def unfold(quads):
    (uu, uv), (vu, vv) = quads
    rows_u = jnp.concatenate([uu + uv, uu - uv], axis=1)
    rows_v = jnp.concatenate([vu + vv, vu - vv], axis=1)
    return jnp.concatenate([rows_u + rows_v, rows_u - rows_v], axis=0)


def two_sided(quads_re, quads_im, tables, left, right):
    half = quads_re[0][0].shape[0]
    lefts = []
    for p in range(2):
        z = jnp.concatenate(
            [jnp.concatenate(quads_re[p], axis=1), jnp.concatenate(quads_im[p], axis=1)], axis=0
        )
        z_hi, z_lo = split(z)
        m_hi, m_lo = tables[left + p, 0], tables[left + p, 1]
        lefts.append(
            dot(
                jnp.concatenate([m_hi, m_hi, m_lo], axis=1),
                jnp.concatenate([z_hi, z_lo, z_hi], axis=0),
            )
        )
    out_re = [[None, None], [None, None]]
    out_im = [[None, None], [None, None]]
    for q in range(2):
        cols = slice(q * half, (q + 1) * half)
        v = jnp.concatenate(
            [jnp.concatenate([w[:half, cols], w[half:, cols]], axis=1) for w in lefts], axis=0
        )
        v_hi, v_lo = split(v)
        m_hi, m_lo = tables[right + q, 0], tables[right + q, 1]
        y = dot(
            jnp.concatenate([v_hi, v_hi, v_lo], axis=1),
            jnp.concatenate([m_hi, m_lo, m_hi], axis=0),
        )
        for p in range(2):
            out_re[p][q] = y[p * half : (p + 1) * half, :half]
            out_im[p][q] = y[p * half : (p + 1) * half, half:]
    return out_re, out_im


def whole(quads):
    return jnp.concatenate([jnp.concatenate(r, axis=1) for r in quads], axis=0)


def quarters(x):
    half = x.shape[0] // 2
    return [(r[:, :half], r[:, half:]) for r in (x[:half], x[half:])]


LANES = 128
ROWS = 8
MIB = 1024 * 1024


def places(top, edge, side):
    first = pl.multiple_of(top // ROWS * ROWS, ROWS)
    start = pl.multiple_of(edge // LANES * LANES, LANES)
    return [(pl.ds(first, side + ROWS), pl.ds(pl.multiple_of(start + k * LANES, LANES), LANES)) for k in range(3)]


def iotas(rows):
    return (
        lax.broadcasted_iota(jnp.int32, (ROWS, LANES), 0),
        lax.broadcasted_iota(jnp.int32, (rows, LANES), 1),
    )


def window(ext, at, top, edge, side):
    down, over = top % ROWS, edge % LANES
    row, lane = iotas(side + ROWS)
    x = [ext[(*at, *place)] for place in places(top, edge, side)]
    blocks = [jnp.where(lane >= over, x[0], x[2]), x[1]]
    return jnp.concatenate(
        [
            jnp.concatenate([jnp.where(row >= down, y[:ROWS], y[side:]), y[ROWS:side]], axis=0)
            for y in blocks
        ],
        axis=1,
    )


def add_window(grid, at, top, edge, value):
    side = value.shape[0]
    down, over = top % ROWS, edge % LANES
    row, lane = iotas(side)
    x, y = value[:, :LANES], value[:, LANES:]
    blocks = [jnp.where(lane >= over, x, 0.0), y, jnp.where(lane < over, x, 0.0)]
    for place, block in zip(places(top, edge, side), blocks):
        low = jnp.where(row >= down, block[:ROWS], 0.0)
        high = jnp.where(row < down, block[:ROWS], 0.0)
        here = (*at, *place)
        grid[here] = grid[here] + jnp.concatenate([low, block[ROWS:], high], axis=0)


def turned(x, down, over):
    side = x.shape[0]
    tiles = side // ROWS
    row = lax.broadcasted_iota(jnp.int32, (tiles, ROWS, LANES), 1)
    lane = lax.broadcasted_iota(jnp.int32, (side, LANES), 1)
    blocks = []
    for k in range(2):
        y = pltpu.roll(x[:, k * LANES : (k + 1) * LANES].reshape(tiles, ROWS, LANES), down, 1)
        before = jnp.concatenate([y[-1:], y[:-1]], axis=0)
        blocks.append(pltpu.roll(jnp.where(row >= down, y, before).reshape(side, LANES), over, 1))
    return jnp.concatenate([jnp.where(lane >= over, blocks[k], blocks[1 - k]) for k in range(2)], axis=1)


def turned_back(x, down, over):
    side = x.shape[0]
    tiles = side // ROWS
    row = lax.broadcasted_iota(jnp.int32, (tiles, ROWS, LANES), 1)
    lane = lax.broadcasted_iota(jnp.int32, (side, LANES), 1)
    blocks = [pltpu.roll(x[:, k * LANES : (k + 1) * LANES], (LANES - over) % LANES, 1) for k in range(2)]
    out = []
    for k in range(2):
        y = jnp.where(lane < LANES - over, blocks[k], blocks[1 - k]).reshape(tiles, ROWS, LANES)
        y = pltpu.roll(y, (ROWS - down) % ROWS, 1)
        following = jnp.concatenate([y[1:], y[:1]], axis=0)
        out.append(jnp.where(row < ROWS - down, y, following).reshape(side, LANES))
    return jnp.concatenate(out, axis=1)


def times(x, y):
    return x[0] * y[0] - x[1] * y[1], x[0] * y[1] + x[1] * y[0]


def times_conj(x, y):
    return x[0] * y[0] + x[1] * y[1], x[0] * y[1] - x[1] * y[0]


def gradient_kernel(
    offsets, counts, obj, right0, right1, low_left, low_right, corner, middle, probe, measured, tables,
    main_out, right0_out, right1_out, low_left_out, low_right_out, corner_out, probe_out, ext, grid,
):
    height, width = obj.shape[2:]
    side = probe.shape[1]
    ext[:, :, :height, :width] = obj[...]
    ext[:, 0, :height, width:] = right0[...]
    ext[:, 1, :height, width:] = right1[...]
    ext[:, :, height:, :side] = low_left[...]
    ext[:, :, height:, side:width] = low_right[...]
    ext[:, :, height:, width:] = corner[...] + middle[...]
    grid[...] = jnp.zeros_like(grid)
    probe_out[...] = jnp.zeros_like(probe_out)

    def visit(slots):
        places_of = [(offsets[slot, 0], offsets[slot, 1]) for slot in slots]
        turns = [(top % ROWS, edge % LANES) for top, edge in places_of]
        p = [[turned(probe[i], *turn) for i in range(2)] for turn in turns]
        a = [[window(ext, (i, 0), *at, side) for i in range(2)] for at in places_of]
        psi = [times(x, y) for x, y in zip(p, a)]
        y = [two_sided(fold(x[0]), fold(x[1]), tables, 0, 2) for x in psi]
        phi = [[unfold(part) for part in x] for x in y]
        b = [[window(ext, (i, 1), *at, side) for i in range(2)] for at in places_of]
        psi = [times(x, z) for x, z in zip(phi, b)]
        y = [two_sided(fold(x[0]), fold(x[1]), tables, 4, 6) for x in psi]
        far = [[whole(part) for part in x] for x in y]
        misfit = [2.0 * (x[0] * x[0] + x[1] * x[1] - measured[slot]) for x, slot in zip(far, slots)]
        y = [two_sided(quarters(m * x[0]), quarters(m * x[1]), tables, 6, 4) for m, x in zip(misfit, far)]
        d = [[unfold(part) for part in x] for x in y]
        e = [times_conj(x, z) for x, z in zip(b, d)]
        y = [two_sided(fold(x[0]), fold(x[1]), tables, 2, 0) for x in e]
        for at, x, z in zip(places_of, phi, d):
            for i, value in enumerate(times_conj(x, z)):
                add_window(grid, (i, 1), *at, value)
        d = [[unfold(part) for part in x] for x in y]
        for at, x, z in zip(places_of, p, d):
            for i, value in enumerate(times_conj(x, z)):
                add_window(grid, (i, 0), *at, value)
        for turn, x, z in zip(turns, a, d):
            for i, value in enumerate(times_conj(x, z)):
                probe_out[i] += turned_back(value, *turn)

    live = jnp.minimum(counts[0], measured.shape[0])

    def visit_two(pair, carry):
        visit((2 * pair, 2 * pair + 1))
        return carry

    lax.fori_loop(0, live // 2, visit_two, 0)

    @pl.when(live % 2 == 1)
    def _():
        visit((live - 1,))

    main_out[...] = grid[:, :, :height, :width]
    right0_out[...] = grid[:, 0, :height, width:]
    right1_out[...] = grid[:, 1, :height, width:]
    low_left_out[...] = grid[:, :, height:, :side]
    low_right_out[...] = grid[:, :, height:, side:width]
    corner_out[...] = grid[:, :, height:, width:]


def side_kernel(held, left0, middle0, left1, out):
    for layer, terms in enumerate(((left0, middle0), (left1,))):

        @pl.when(layer == pl.program_id(1))
        def _():
            out[...] = held[...] + sum(term[...] for term in terms)


def top_kernel(own_corner, held, corner, low_left, low_right, out):
    side = low_right.shape[1]
    middle = jnp.where(own_corner[0] == 1, corner[...], 0.0)
    out[:, :side] = held[:, :side] + (low_left[...] + middle)
    out[:, side:] = held[:, side:] + low_right[...]


def order_kernel(measured, picks, out):
    def parts(x):
        high = x.astype(jnp.bfloat16)
        rest = x - high.astype(jnp.float32)
        return (high, *split(rest))

    rows = sum(dot(picks[...], x) for x in parts(measured[...]))
    out[...] = sum(
        lax.dot_general(x, picks[...], (((1,), (1,)), ((), ())), preferred_element_type=jnp.float32)
        for x in parts(rows)
    )


def add_kernel(*refs):
    *terms, out = refs
    out[...] = sum(term[...] for term in terms)


def own_kernel(mine, value, own, other):
    own[...] = value[mine[0]]
    other[...] = value[1 - mine[0]]


BESIDE = pl.CostEstimate(flops=0, bytes_accessed=400 * MIB, transcendentals=0)
SMALL = pl.CostEstimate(flops=0, bytes_accessed=1024, transcendentals=0)


def fixed(shape):
    return pl.BlockSpec(shape, lambda q: (0,) * len(shape))


def per_slot(*shape):
    return pl.BlockSpec((None, *shape), lambda q: (q,) + (0,) * len(shape))


SCALARS = pl.BlockSpec(memory_space=pltpu.SMEM)


def struct(*shape):
    return jax.ShapeDtypeStruct(shape, jnp.float32)


def moved(shard, pairs):
    cols = lax.axis_size("col")
    flat = [(a * cols + b, c * cols + d) for (a, b), (c, d) in pairs]
    return lax.ppermute(shard, ("row", "col"), flat)


def along_columns(shard, by, middle):
    rows, cols = lax.axis_size("row"), lax.axis_size("col")
    cut, end = cols // 2, 0 if by < 0 else cols - 1
    first, second = (cut, cut - 1) if by < 0 else (cut - 1, cut)
    pairs = [(c, c + by) for c in range(cols) if c not in (first, end)]
    pairs += [(first, second)] if middle == "direct" else []
    pairs = [((r, c), (r, to)) for r in range(rows) for c, to in pairs]
    pairs += [((r ^ 1, end), (r, second)) for r in range(rows)] if middle == "relay" else []
    pairs += [((r, first), (r + 1, second)) for r in range(rows - 1)] if middle == "diagonal" else []
    return moved(shard, pairs)


def to_end(shard, by):
    rows, cols = lax.axis_size("row"), lax.axis_size("col")
    first, end = (cols // 2, 0) if by < 0 else (cols // 2 - 1, cols - 1)
    return moved(shard, [((r, first), (r ^ 1, end)) for r in range(rows)])


def across_middle(shard, by, down):
    rows, cols = lax.axis_size("row"), lax.axis_size("col")
    first, second = (cols // 2, cols // 2 - 1) if by < 0 else (cols // 2 - 1, cols // 2)
    return moved(shard, [((r, first), (r + down, second)) for r in range(rows) if 0 <= r + down < rows])


def after(first, then):
    return lax.optimization_barrier((first, then))


PHYSICAL = {"core": 2, "y": 4, "x": 4, "z_lo": 2, "z_hi": 2}


def physical(r, c):
    return {"x": r // 2, "z_lo": r % 2, "z_hi": c // 8, "y": c // 2 % 4, "core": c % 2}


def exchanged(shard, **flips):
    pairs = []
    for r in range(lax.axis_size("row")):
        for c in range(lax.axis_size("col")):
            to = physical(r, c)
            for which, flip in flips.items():
                to[which] ^= flip
            pairs.append(((r, c), (to["x"] * 2 + to["z_lo"], to["z_hi"] * 8 + to["y"] * 2 + to["core"])))
    return moved(shard, pairs)


def added(*terms):
    return pl.pallas_call(add_kernel, out_shape=struct(*terms[0].shape), cost_estimate=BESIDE)(*terms)


def halved(bit, value):
    return pl.pallas_call(
        own_kernel, in_specs=[SCALARS, pl.BlockSpec(memory_space=pltpu.VMEM)],
        out_shape=[struct(*value.shape[1:])] * 2, cost_estimate=BESIDE,
    )(bit.reshape(1), value)


def split_rows(value, bit):
    first, second = value[: value.shape[0] // 2], value[value.shape[0] // 2 :]
    return jnp.where(bit == 1, second, first), jnp.where(bit == 1, first, second)


def joined(bit, own, other):
    return jnp.concatenate([jnp.where(bit == 1, other, own), jnp.where(bit == 1, own, other)], axis=0)


def per_device(object_field, probe, measured, offsets, counts):
    _, layers, height, width = object_field.shape
    side = probe.shape[1]
    slots = measured.shape[0]
    cols = lax.axis_size("col")
    cut = cols // 2

    here = lax.axis_index("col")
    wait = lax.optimization_barrier
    low_left = passed_along(object_field[:, :, :side, :side], "row", -1)
    low_right = passed_along(object_field[:, :, :side, side:], "row", -1)
    rim = [object_field[:, i, :, :side] for i in range(layers)]
    half = to_end(rim[1], -1)
    right0 = along_columns(rim[0], -1, "direct")
    right1 = along_columns(jnp.where(here == 0, half, rim[1]), -1, "relay")
    middle = across_middle(object_field[:, :, :side, :side], -1, -1)
    order = np.concatenate([np.arange(0, side, 2), np.arange(1, side, 2)])
    picks = jnp.asarray(np.eye(side)[order].astype(ml_dtypes.bfloat16))
    pattern = pl.pallas_call(
        order_kernel, grid=(slots,), in_specs=[per_slot(side, side), fixed((side, side))],
        out_specs=per_slot(side, side), out_shape=struct(slots, side, side), cost_estimate=BESIDE,
    )(measured, picks)
    pattern, low_left = wait((pattern, low_left))
    corner = along_columns(low_left, -1, "nothing")

    vmem = pl.BlockSpec(memory_space=pltpu.VMEM)
    extended = pltpu.VMEM((2, layers, height + side, width + side), jnp.float32)
    main, rim0, rim1, low_left, low_right, corner, probe_terms = pl.pallas_call(
        gradient_kernel,
        in_specs=[SCALARS, SCALARS] + [vmem] * 10,
        out_specs=[vmem] * 7,
        out_shape=[
            struct(2, layers, height, width), struct(2, height, side), struct(2, height, side),
            *[struct(2, layers, side, side)] * 3, struct(2, side, side),
        ],
        scratch_shapes=[extended, extended],
        compiler_params=pltpu.CompilerParams(vmem_limit_bytes=60 * MIB),
        cost_estimate=BESIDE,
    )(
        offsets, counts, object_field, right0, right1, low_left, low_right, corner, middle, probe, pattern,
        jnp.asarray(make_tables(side)),
    )

    me = physical(lax.axis_index("row"), lax.axis_index("col"))
    low_bit, high_bit = me["y"] % 2 ^ me["y"] // 2, me["y"] // 2
    down_right = passed_along(low_right, "row", 1)
    from_corner = along_columns(corner, 1, "diagonal")
    half = to_end(rim1, 1)
    own, other = halved(me["core"], probe_terms)
    own, other = split_rows(own + exchanged(other, core=1), low_bit)
    own, other = split_rows(own + exchanged(other, y=1), high_bit)
    from_left0 = along_columns(rim0, 1, "nothing")
    arrived, down_right, from_left0, rim0 = wait((exchanged(other, y=3), down_right, from_left0, rim0))
    over_middle = across_middle(rim0, 1, 0)
    from_left1 = along_columns(jnp.where(here == cols - 1, half, rim1), 1, "relay")
    share = own + arrived
    share = share + exchanged(share, x=1)
    share = share + exchanged(share, x=3)
    share = share + exchanged(share, z_lo=1)
    own_corner = here == cut
    passed_on = low_left + jnp.where(own_corner, 0.0, from_corner)
    arrived, over_middle, from_left1, passed_on = wait(
        (exchanged(share, z_lo=1, z_hi=1), over_middle, from_left1, passed_on)
    )
    down_left = passed_along(passed_on, "row", 1)
    share = added(share, arrived)
    share = joined(high_bit, share, exchanged(share, y=3))
    share = joined(low_bit, share, exchanged(share, y=1))
    edge = pl.BlockSpec((None, height, side), lambda i, j: (i, 0, 0))
    corner = pl.BlockSpec((None, None, side, side), lambda i, j: (i, j, 0, 0))
    upper = pl.BlockSpec((None, None, side, width), lambda i, j: (i, j, 0, 0))
    left = pl.BlockSpec((None, None, height, side), lambda i, j: (i, j, 0, 0))
    result = pl.pallas_call(
        side_kernel, grid=(2, layers), in_specs=[left, edge, edge, edge], out_specs=left,
        out_shape=struct(*object_field.shape), input_output_aliases={0: 0}, cost_estimate=SMALL,
    )(main, from_left0, over_middle, from_left1)
    share, down_left, result = wait((share, down_left, result))
    probe_grad = joined(me["core"], share, exchanged(share, core=1)).reshape(probe.shape)
    result = pl.pallas_call(
        top_kernel, grid=(2, layers), in_specs=[SCALARS, upper, corner, corner, corner], out_specs=upper,
        out_shape=struct(*object_field.shape), input_output_aliases={1: 0},
    )(own_corner.astype(jnp.int32).reshape(1), result, from_corner, down_left, down_right)
    return (result, probe_grad)


def solution(mesh):
    placed = (
        P(None, None, "row", "col"),
        P(),
        P(("row", "col"), None, None),
        P(("row", "col"), None),
        P(("row", "col")),
    )
    return jax.shard_map(
        per_device,
        mesh=mesh,
        in_specs=placed,
        out_specs=(P(None, None, "row", "col"), P()),
        check_vma=False,
    )
```

```python
import math

import jax
import jax.numpy as jnp
import ml_dtypes
import numpy as np
from jax import lax
from jax.experimental import pallas as pl
from jax.experimental.pallas import tpu as pltpu
from jax.sharding import PartitionSpec as P

fresnel = 40.0


def passed_along(shard, axis, by):
    length = lax.axis_size(axis)
    pairs = [(i, i + by) for i in range(length) if 0 <= i + by < length]
    return lax.ppermute(shard, axis, pairs)


def real_form(matrix):
    return np.block([[matrix.real, -matrix.imag], [matrix.imag, matrix.real]])


def make_tables(side):
    half = side // 2
    index = np.arange(side)
    dft = np.exp(-2j * np.pi * ((index[:, None] * index[None, :]) % side) / side) / math.sqrt(side)
    freqs = (index + half) % side - half
    chirp = np.exp(1j * fresnel * np.pi * (freqs * freqs) / (side * side))
    circulant = (dft.conj() * chirp[None, :]) @ dft
    near, far = circulant[:half, :half], circulant[:half, half:]
    mats = [real_form((near + far) / 2), real_form((near - far) / 2)]
    mats += [real_form(dft[0::2, :half]), real_form(dft[1::2, :half])]
    full = np.stack([mats[0], mats[1], mats[0].T, mats[1].T, mats[2], mats[3], mats[2].T, mats[3].T])
    full = full.astype(np.float32)
    high = full.astype(ml_dtypes.bfloat16)
    low = (full - high.astype(np.float32)).astype(ml_dtypes.bfloat16)
    return np.stack([high, low], axis=1)


def split(x):
    high = x.astype(jnp.bfloat16)
    return high, (x - high.astype(jnp.float32)).astype(jnp.bfloat16)


def dot(a, b):
    return jnp.dot(a, b, preferred_element_type=jnp.float32)


def fold(x):
    half = x.shape[0] // 2
    rows = (x[:half] + x[half:], x[:half] - x[half:])
    return [(r[:, :half] + r[:, half:], r[:, :half] - r[:, half:]) for r in rows]


def unfold(quads):
    (uu, uv), (vu, vv) = quads
    rows_u = jnp.concatenate([uu + uv, uu - uv], axis=1)
    rows_v = jnp.concatenate([vu + vv, vu - vv], axis=1)
    return jnp.concatenate([rows_u + rows_v, rows_u - rows_v], axis=0)


def two_sided(quads_re, quads_im, tables, left, right):
    half = quads_re[0][0].shape[0]
    lefts = []
    for p in range(2):
        z = jnp.concatenate(
            [jnp.concatenate(quads_re[p], axis=1), jnp.concatenate(quads_im[p], axis=1)], axis=0
        )
        z_hi, z_lo = split(z)
        m_hi, m_lo = tables[left + p, 0], tables[left + p, 1]
        lefts.append(
            dot(
                jnp.concatenate([m_hi, m_hi, m_lo], axis=1),
                jnp.concatenate([z_hi, z_lo, z_hi], axis=0),
            )
        )
    out_re = [[None, None], [None, None]]
    out_im = [[None, None], [None, None]]
    for q in range(2):
        cols = slice(q * half, (q + 1) * half)
        v = jnp.concatenate(
            [jnp.concatenate([w[:half, cols], w[half:, cols]], axis=1) for w in lefts], axis=0
        )
        v_hi, v_lo = split(v)
        m_hi, m_lo = tables[right + q, 0], tables[right + q, 1]
        y = dot(
            jnp.concatenate([v_hi, v_hi, v_lo], axis=1),
            jnp.concatenate([m_hi, m_lo, m_hi], axis=0),
        )
        for p in range(2):
            out_re[p][q] = y[p * half : (p + 1) * half, :half]
            out_im[p][q] = y[p * half : (p + 1) * half, half:]
    return out_re, out_im


def whole(quads):
    return jnp.concatenate([jnp.concatenate(r, axis=1) for r in quads], axis=0)


def quarters(x):
    half = x.shape[0] // 2
    return [(r[:, :half], r[:, half:]) for r in (x[:half], x[half:])]


LANES = 128
ROWS = 8
MIB = 1024 * 1024


def places(top, edge, side):
    first = pl.multiple_of(top // ROWS * ROWS, ROWS)
    start = pl.multiple_of(edge // LANES * LANES, LANES)
    return [(pl.ds(first, side + ROWS), pl.ds(pl.multiple_of(start + k * LANES, LANES), LANES)) for k in range(3)]


def iotas(rows):
    return (
        lax.broadcasted_iota(jnp.int32, (ROWS, LANES), 0),
        lax.broadcasted_iota(jnp.int32, (rows, LANES), 1),
    )


def window(ext, at, top, edge, side):
    down, over = top % ROWS, edge % LANES
    row, lane = iotas(side + ROWS)
    x = [ext[(*at, *place)] for place in places(top, edge, side)]
    blocks = [jnp.where(lane >= over, x[0], x[2]), x[1]]
    return jnp.concatenate(
        [
            jnp.concatenate([jnp.where(row >= down, y[:ROWS], y[side:]), y[ROWS:side]], axis=0)
            for y in blocks
        ],
        axis=1,
    )


def add_window(grid, at, top, edge, value):
    side = value.shape[0]
    down, over = top % ROWS, edge % LANES
    row, lane = iotas(side)
    x, y = value[:, :LANES], value[:, LANES:]
    blocks = [jnp.where(lane >= over, x, 0.0), y, jnp.where(lane < over, x, 0.0)]
    for place, block in zip(places(top, edge, side), blocks):
        low = jnp.where(row >= down, block[:ROWS], 0.0)
        high = jnp.where(row < down, block[:ROWS], 0.0)
        here = (*at, *place)
        grid[here] = grid[here] + jnp.concatenate([low, block[ROWS:], high], axis=0)


def turned(x, down, over):
    side = x.shape[0]
    tiles = side // ROWS
    row = lax.broadcasted_iota(jnp.int32, (tiles, ROWS, LANES), 1)
    lane = lax.broadcasted_iota(jnp.int32, (side, LANES), 1)
    blocks = []
    for k in range(2):
        y = pltpu.roll(x[:, k * LANES : (k + 1) * LANES].reshape(tiles, ROWS, LANES), down, 1)
        before = jnp.concatenate([y[-1:], y[:-1]], axis=0)
        blocks.append(pltpu.roll(jnp.where(row >= down, y, before).reshape(side, LANES), over, 1))
    return jnp.concatenate([jnp.where(lane >= over, blocks[k], blocks[1 - k]) for k in range(2)], axis=1)


def turned_back(x, down, over):
    side = x.shape[0]
    tiles = side // ROWS
    row = lax.broadcasted_iota(jnp.int32, (tiles, ROWS, LANES), 1)
    lane = lax.broadcasted_iota(jnp.int32, (side, LANES), 1)
    blocks = [pltpu.roll(x[:, k * LANES : (k + 1) * LANES], (LANES - over) % LANES, 1) for k in range(2)]
    out = []
    for k in range(2):
        y = jnp.where(lane < LANES - over, blocks[k], blocks[1 - k]).reshape(tiles, ROWS, LANES)
        y = pltpu.roll(y, (ROWS - down) % ROWS, 1)
        following = jnp.concatenate([y[1:], y[:1]], axis=0)
        out.append(jnp.where(row < ROWS - down, y, following).reshape(side, LANES))
    return jnp.concatenate(out, axis=1)


def times(x, y):
    return x[0] * y[0] - x[1] * y[1], x[0] * y[1] + x[1] * y[0]


def times_conj(x, y):
    return x[0] * y[0] + x[1] * y[1], x[0] * y[1] - x[1] * y[0]


def gradient_kernel(
    offsets, counts, obj, right0, right1, low_left, low_right, corner, middle, probe, measured, tables,
    main_out, right0_out, right1_out, low_left_out, low_right_out, corner_out, probe_out, ext, grid,
):
    height, width = obj.shape[2:]
    side = probe.shape[1]
    ext[:, :, :height, :width] = obj[...]
    ext[:, 0, :height, width:] = right0[...]
    ext[:, 1, :height, width:] = right1[...]
    ext[:, :, height:, :side] = low_left[...]
    ext[:, :, height:, side:width] = low_right[...]
    ext[:, :, height:, width:] = corner[...] + middle[...]
    grid[...] = jnp.zeros_like(grid)
    probe_out[...] = jnp.zeros_like(probe_out)

    def visit(slots):
        places_of = [(offsets[slot, 0], offsets[slot, 1]) for slot in slots]
        turns = [(top % ROWS, edge % LANES) for top, edge in places_of]
        p = [[turned(probe[i], *turn) for i in range(2)] for turn in turns]
        a = [[window(ext, (i, 0), *at, side) for i in range(2)] for at in places_of]
        psi = [times(x, y) for x, y in zip(p, a)]
        y = [two_sided(fold(x[0]), fold(x[1]), tables, 0, 2) for x in psi]
        phi = [[unfold(part) for part in x] for x in y]
        b = [[window(ext, (i, 1), *at, side) for i in range(2)] for at in places_of]
        psi = [times(x, z) for x, z in zip(phi, b)]
        y = [two_sided(fold(x[0]), fold(x[1]), tables, 4, 6) for x in psi]
        far = [[whole(part) for part in x] for x in y]
        misfit = [2.0 * (x[0] * x[0] + x[1] * x[1] - measured[slot]) for x, slot in zip(far, slots)]
        y = [two_sided(quarters(m * x[0]), quarters(m * x[1]), tables, 6, 4) for m, x in zip(misfit, far)]
        d = [[unfold(part) for part in x] for x in y]
        e = [times_conj(x, z) for x, z in zip(b, d)]
        y = [two_sided(fold(x[0]), fold(x[1]), tables, 2, 0) for x in e]
        for at, x, z in zip(places_of, phi, d):
            for i, value in enumerate(times_conj(x, z)):
                add_window(grid, (i, 1), *at, value)
        d = [[unfold(part) for part in x] for x in y]
        for at, x, z in zip(places_of, p, d):
            for i, value in enumerate(times_conj(x, z)):
                add_window(grid, (i, 0), *at, value)
        for turn, x, z in zip(turns, a, d):
            for i, value in enumerate(times_conj(x, z)):
                probe_out[i] += turned_back(value, *turn)

    live = jnp.minimum(counts[0], measured.shape[0])

    def visit_two(pair, carry):
        visit((2 * pair, 2 * pair + 1))
        return carry

    lax.fori_loop(0, live // 2, visit_two, 0)

    @pl.when(live % 2 == 1)
    def _():
        visit((live - 1,))

    main_out[...] = grid[:, :, :height, :width]
    right0_out[...] = grid[:, 0, :height, width:]
    right1_out[...] = grid[:, 1, :height, width:]
    low_left_out[...] = grid[:, :, height:, :side]
    low_right_out[...] = grid[:, :, height:, side:width]
    corner_out[...] = grid[:, :, height:, width:]


def side_kernel(held, left0, middle0, left1, out):
    for layer, terms in enumerate(((left0, middle0), (left1,))):

        @pl.when(layer == pl.program_id(1))
        def _():
            out[...] = held[...] + sum(term[...] for term in terms)


def top_kernel(own_corner, held, corner, low_left, low_right, out):
    side = low_right.shape[1]
    middle = jnp.where(own_corner[0] == 1, corner[...], 0.0)
    out[:, :side] = held[:, :side] + (low_left[...] + middle)
    out[:, side:] = held[:, side:] + low_right[...]


def order_kernel(measured, picks, out):
    def parts(x):
        high = x.astype(jnp.bfloat16)
        rest = x - high.astype(jnp.float32)
        return (high, *split(rest))

    rows = sum(dot(picks[...], x) for x in parts(measured[...]))
    out[...] = sum(
        lax.dot_general(x, picks[...], (((1,), (1,)), ((), ())), preferred_element_type=jnp.float32)
        for x in parts(rows)
    )


def add_kernel(*refs):
    *terms, out = refs
    out[...] = sum(term[...] for term in terms)


def own_kernel(mine, value, own, other):
    own[...] = value[mine[0]]
    other[...] = value[1 - mine[0]]


BESIDE = pl.CostEstimate(flops=0, bytes_accessed=400 * MIB, transcendentals=0)
SMALL = pl.CostEstimate(flops=0, bytes_accessed=1024, transcendentals=0)


def fixed(shape):
    return pl.BlockSpec(shape, lambda q: (0,) * len(shape))


def per_slot(*shape):
    return pl.BlockSpec((None, *shape), lambda q: (q,) + (0,) * len(shape))


SCALARS = pl.BlockSpec(memory_space=pltpu.SMEM)


def struct(*shape):
    return jax.ShapeDtypeStruct(shape, jnp.float32)


def moved(shard, pairs):
    cols = lax.axis_size("col")
    flat = [(a * cols + b, c * cols + d) for (a, b), (c, d) in pairs]
    return lax.ppermute(shard, ("row", "col"), flat)


def along_columns(shard, by, middle):
    rows, cols = lax.axis_size("row"), lax.axis_size("col")
    cut, end = cols // 2, 0 if by < 0 else cols - 1
    first, second = (cut, cut - 1) if by < 0 else (cut - 1, cut)
    pairs = [(c, c + by) for c in range(cols) if c not in (first, end)]
    pairs += [(first, second)] if middle == "direct" else []
    pairs = [((r, c), (r, to)) for r in range(rows) for c, to in pairs]
    pairs += [((r ^ 1, end), (r, second)) for r in range(rows)] if middle == "relay" else []
    pairs += [((r, first), (r + 1, second)) for r in range(rows - 1)] if middle == "diagonal" else []
    return moved(shard, pairs)


def to_end(shard, by):
    rows, cols = lax.axis_size("row"), lax.axis_size("col")
    first, end = (cols // 2, 0) if by < 0 else (cols // 2 - 1, cols - 1)
    return moved(shard, [((r, first), (r ^ 1, end)) for r in range(rows)])


def across_middle(shard, by, down):
    rows, cols = lax.axis_size("row"), lax.axis_size("col")
    first, second = (cols // 2, cols // 2 - 1) if by < 0 else (cols // 2 - 1, cols // 2)
    return moved(shard, [((r, first), (r + down, second)) for r in range(rows) if 0 <= r + down < rows])


def after(first, then):
    return lax.optimization_barrier((first, then))


PHYSICAL = {"core": 2, "y": 4, "x": 4, "z_lo": 2, "z_hi": 2}


def physical(r, c):
    return {"x": r // 2, "z_lo": r % 2, "z_hi": c // 8, "y": c // 2 % 4, "core": c % 2}


def exchanged(shard, **flips):
    pairs = []
    for r in range(lax.axis_size("row")):
        for c in range(lax.axis_size("col")):
            to = physical(r, c)
            for which, flip in flips.items():
                to[which] ^= flip
            pairs.append(((r, c), (to["x"] * 2 + to["z_lo"], to["z_hi"] * 8 + to["y"] * 2 + to["core"])))
    return moved(shard, pairs)


def added(*terms):
    return pl.pallas_call(add_kernel, out_shape=struct(*terms[0].shape), cost_estimate=BESIDE)(*terms)


def halved(bit, value):
    return pl.pallas_call(
        own_kernel, in_specs=[SCALARS, pl.BlockSpec(memory_space=pltpu.VMEM)],
        out_shape=[struct(*value.shape[1:])] * 2, cost_estimate=BESIDE,
    )(bit.reshape(1), value)


def split_rows(value, bit):
    first, second = value[: value.shape[0] // 2], value[value.shape[0] // 2 :]
    return jnp.where(bit == 1, second, first), jnp.where(bit == 1, first, second)


def joined(bit, own, other):
    return jnp.concatenate([jnp.where(bit == 1, other, own), jnp.where(bit == 1, own, other)], axis=0)


def per_device(object_field, probe, measured, offsets, counts):
    _, layers, height, width = object_field.shape
    side = probe.shape[1]
    slots = measured.shape[0]
    cols = lax.axis_size("col")
    cut = cols // 2

    here = lax.axis_index("col")
    wait = lax.optimization_barrier
    low_left = passed_along(object_field[:, :, :side, :side], "row", -1)
    low_right = passed_along(object_field[:, :, :side, side:], "row", -1)
    rim = [object_field[:, i, :, :side] for i in range(layers)]
    half = to_end(rim[1], -1)
    right0 = along_columns(rim[0], -1, "direct")
    right1 = along_columns(jnp.where(here == 0, half, rim[1]), -1, "relay")
    middle = across_middle(object_field[:, :, :side, :side], -1, -1)
    order = np.concatenate([np.arange(0, side, 2), np.arange(1, side, 2)])
    picks = jnp.asarray(np.eye(side)[order].astype(ml_dtypes.bfloat16))
    pattern = pl.pallas_call(
        order_kernel, grid=(slots,), in_specs=[per_slot(side, side), fixed((side, side))],
        out_specs=per_slot(side, side), out_shape=struct(slots, side, side), cost_estimate=BESIDE,
    )(measured, picks)
    pattern, low_left = wait((pattern, low_left))
    corner = along_columns(low_left, -1, "nothing")

    vmem = pl.BlockSpec(memory_space=pltpu.VMEM)
    extended = pltpu.VMEM((2, layers, height + side, width + side), jnp.float32)
    main, rim0, rim1, low_left, low_right, corner, probe_terms = pl.pallas_call(
        gradient_kernel,
        in_specs=[SCALARS, SCALARS] + [vmem] * 10,
        out_specs=[vmem] * 7,
        out_shape=[
            struct(2, layers, height, width), struct(2, height, side), struct(2, height, side),
            *[struct(2, layers, side, side)] * 3, struct(2, side, side),
        ],
        scratch_shapes=[extended, extended],
        compiler_params=pltpu.CompilerParams(vmem_limit_bytes=60 * MIB),
        cost_estimate=BESIDE,
    )(
        offsets, counts, object_field, right0, right1, low_left, low_right, corner, middle, probe, pattern,
        jnp.asarray(make_tables(side)),
    )

    me = physical(lax.axis_index("row"), lax.axis_index("col"))
    low_bit, high_bit = me["y"] % 2 ^ me["y"] // 2, me["y"] // 2
    down_right = passed_along(low_right, "row", 1)
    from_corner = along_columns(corner, 1, "diagonal")
    half = to_end(rim1, 1)
    own, other = halved(me["core"], probe_terms)
    own, other = split_rows(own + exchanged(other, core=1), low_bit)
    own, other = split_rows(own + exchanged(other, y=1), high_bit)
    from_left0 = along_columns(rim0, 1, "nothing")
    relayed = jnp.where(here == cols - 1, half, rim1)
    arrived, down_right, from_left0, rim0, relayed = wait(
        (exchanged(other, y=3), down_right, from_left0, rim0, relayed)
    )
    over_middle = across_middle(rim0, 1, 0)
    from_left1 = along_columns(relayed, 1, "relay")
    share = own + arrived
    share = share + exchanged(share, x=1)
    share = share + exchanged(share, x=3)
    share = share + exchanged(share, z_lo=1)
    own_corner = here == cut
    passed_on = low_left + jnp.where(own_corner, 0.0, from_corner)
    arrived, over_middle, from_left1, passed_on = wait(
        (exchanged(share, z_lo=1, z_hi=1), over_middle, from_left1, passed_on)
    )
    down_left = passed_along(passed_on, "row", 1)
    share = added(share, arrived)
    share = joined(high_bit, share, exchanged(share, y=3))
    share = joined(low_bit, share, exchanged(share, y=1))
    edge = pl.BlockSpec((None, height, side), lambda i, j: (i, 0, 0))
    corner = pl.BlockSpec((None, None, side, side), lambda i, j: (i, j, 0, 0))
    upper = pl.BlockSpec((None, None, side, width), lambda i, j: (i, j, 0, 0))
    left = pl.BlockSpec((None, None, height, side), lambda i, j: (i, j, 0, 0))
    result = pl.pallas_call(
        side_kernel, grid=(2, layers), in_specs=[left, edge, edge, edge], out_specs=left,
        out_shape=struct(*object_field.shape), input_output_aliases={0: 0}, cost_estimate=SMALL,
    )(main, from_left0, over_middle, from_left1)
    share, down_left, result = wait((share, down_left, result))
    probe_grad = joined(me["core"], share, exchanged(share, core=1)).reshape(probe.shape)
    result = pl.pallas_call(
        top_kernel, grid=(2, layers), in_specs=[SCALARS, upper, corner, corner, corner], out_specs=upper,
        out_shape=struct(*object_field.shape), input_output_aliases={1: 0},
    )(own_corner.astype(jnp.int32).reshape(1), result, from_corner, down_left, down_right)
    return (result, probe_grad)


def solution(mesh):
    placed = (
        P(None, None, "row", "col"),
        P(),
        P(("row", "col"), None, None),
        P(("row", "col"), None),
        P(("row", "col")),
    )
    return jax.shard_map(
        per_device,
        mesh=mesh,
        in_specs=placed,
        out_specs=(P(None, None, "row", "col"), P()),
        check_vma=False,
    )
```
